32 devices in a mesh: facet: 8 (over y, x, core), bl: 4 (over z).
Axes of the slice: x: 2, y: 2, z: 4, core: 2. Of those that a mesh axis runs over, the one named last changes fastest.
Arguments:
- facet_model: bfloat16 [8, 1024, 1024], P('facet', 'bl'), may hold values from -0.005859375 to 0.005859375
- screens: bfloat16 [8, 256, 64, 128], P('facet', 'bl'), may hold values from 0.099609375 to 1.8984375
- observed: float32 [48, 64, 128], P('bl'), may hold values from -24 to 24
- offsets: int32 [48, 2], P('bl'), may hold values from 0 to 4032
- stations: int32 [48, 2], P('bl'), may hold values from 0 to 255
- counts: int32 [4], P('bl'), may hold values from 1 to 12, as said below
Outputs:
- residual_vis: float32 [48, 64, 128], P('bl')
- residual_image: float32 [8, 1024, 1024], P('facet', 'bl')
The draws below stay inside these ranges and needn't reach their ends.
Inputs may be any that keep to these rules, and one draw needn't show every extreme that they name: `counts`: some baseline block has all 12 slots live.
All inputs are finite; a program needn't handle non-finite values.
Results may differ from the reference program's by a relative error of at most 0.0061.
Values may be sent and summed in bfloat16 or wider, within the bound.
A program may use at most 64 MiB of HBM per device.

```python
import math
import jax
import jax.numpy as jnp
from jax import lax

FACET_PX = 1024
G = 64
STATIONS = 256
FGRID = 4
T_DEV = 12
NF = 8
NBLK = 4
TILES = 48
NIMG = 4096


def draw_counts(key, part):
    first_key, second_key = jax.random.split(jax.random.fold_in(key, 11))
    values = jax.random.randint(first_key, (NBLK,), 1, T_DEV + 1)
    fullest = jax.random.randint(second_key, (), 0, NBLK)
    return jnp.where(jnp.arange(NBLK) == fullest, T_DEV, values).astype(jnp.int32)


def with_ends(array, rng, low, largest):
    longest = array.shape.index(max(array.shape))
    spots = []
    for shift in (0, 1):
        where = [jax.random.randint(jax.random.fold_in(rng, axis), (), 0, length) for axis, length in enumerate(array.shape)]
        where[longest] = (where[longest] + shift) % array.shape[longest]
        spots.append(tuple(where))
    return array.at[spots[0]].set(low).at[spots[1]].set(largest)


def levels(stream_key, shape, cuts, low, high):
    level = 1.0
    for axis_at, blocks in cuts:
        draws = jax.random.uniform(jax.random.fold_in(jax.random.fold_in(stream_key, 6), axis_at), (blocks,), jnp.float32, low / len(cuts), high / len(cuts))
        level = level * jnp.repeat(jnp.exp(draws), shape[axis_at] // blocks).reshape((-1,) + (1,) * (len(shape) - 1 - axis_at))
    return level


def gaussian(key, shape, spread, reach, cuts=(), kind=jnp.bfloat16):
    drawn = jax.random.normal(key, shape, jnp.float32) * spread
    if len(cuts) > 0:
        drawn = levels(key, shape, cuts, -0.22, 0.18) * drawn
    return jnp.clip(drawn, min=-reach, max=reach).astype(kind)


def setup_inputs(seed: int = 0) -> dict:
    arg_keys = jax.random.split(jax.random.key(seed), 7)
    facet_model = gaussian(arg_keys[0], (NF, FACET_PX, FACET_PX), (1.0 / FACET_PX), 0.005859375, ((0, 8), (1, 4)))
    screens = jnp.clip(1.0 + 0.18 * jax.random.normal(arg_keys[1], (NF, STATIONS, G, 2 * G), jnp.float32), 0.099609375, 1.8984375).astype(jnp.bfloat16)
    observed = gaussian(arg_keys[2], (TILES, G, 2 * G), 4.0, 24.0, ((0, 4),), jnp.float32)
    offsets = with_ends(jax.random.randint(arg_keys[3], (TILES, 2), 0, NIMG - G + 1), jax.random.fold_in(arg_keys[3], 1), 0, NIMG - G).astype(jnp.int32)
    stations = with_ends(jax.random.randint(arg_keys[4], (TILES, 2), 0, STATIONS), jax.random.fold_in(arg_keys[4], 1), 0, STATIONS - 1).astype(jnp.int32)
    counts = draw_counts(jax.random.fold_in(arg_keys[6], 71), 0)
    return {"facet_model": facet_model, "screens": screens, "observed": observed, "offsets": offsets, "stations": stations, "counts": counts}


def tables(offset_u, offset_v, facet_id, tile_width, facet_cells):
    grid_cells = FGRID * facet_cells
    corner_x = facet_id // FGRID * facet_cells
    corner_y = facet_id % FGRID * facet_cells
    pixel_index = jnp.arange(facet_cells, dtype=jnp.int32)
    cell_index = jnp.arange(tile_width, dtype=jnp.int32)
    phase_u = jnp.mod((offset_u + cell_index)[:, None] * (corner_x + pixel_index)[None, :], grid_cells)
    phase_v = jnp.mod((offset_v + cell_index)[:, None] * (corner_y + pixel_index)[None, :], grid_cells)
    angle_u = phase_u.astype(jnp.float32) * (2.0 * math.pi / grid_cells)
    angle_v = phase_v.astype(jnp.float32) * (2.0 * math.pi / grid_cells)
    tab_u = jnp.concatenate([jnp.cos(angle_u), -jnp.sin(angle_u)], axis=0).astype(jnp.bfloat16)
    table_vertical = jnp.concatenate([jnp.cos(angle_v), jnp.sin(angle_v)], axis=0).astype(jnp.bfloat16)
    return (tab_u, table_vertical)

def half_splits(value):
    half_width = value.shape[-1] // 2
    return (value[..., :half_width], value[..., half_width:])

def complex_times(left_re, left_im, right_re, right_im):
    return (left_re * right_re - left_im * right_im, left_re * right_im + left_im * right_re)

def times_conj(left_re, left_im, right_re, right_im):
    return (left_re * right_re + left_im * right_im, left_im * right_re - left_re * right_im)

def reference(facet_model, screens, observed, offsets, stations, counts):
    tile_width = observed.shape[1]
    facet_cells = facet_model.shape[1]
    tile_total = observed.shape[0]
    per_block = tile_total // counts.shape[0]
    slot_index = jnp.arange(tile_total, dtype=jnp.int32)
    live_mask = slot_index % per_block < jnp.repeat(counts, per_block)
    facet_ids = jnp.arange(NF, dtype=jnp.int32)

    def predict_tile(tile_args):
        tile_offset, tile_couple = tile_args

        def facet_step(running, facet_id):
            tab_u, table_vertical = tables(tile_offset[0], tile_offset[1], facet_id, tile_width, facet_cells)
            upper_portion = jnp.dot(tab_u, facet_model[facet_id], preferred_element_type=jnp.float32).astype(jnp.bfloat16)
            block_groups = jnp.dot(upper_portion, table_vertical.T, preferred_element_type=jnp.float32)
            real_part = block_groups[:tile_width, :tile_width] + block_groups[tile_width:, tile_width:]
            imag_part = block_groups[tile_width:, :tile_width] - block_groups[:tile_width, tile_width:]
            first_station_gain = screens[facet_id, tile_couple[0]].astype(jnp.float32)
            gain_q = screens[facet_id, tile_couple[1]].astype(jnp.float32)
            p_re, p_im = half_splits(first_station_gain)
            q_re, q_im = half_splits(gain_q)
            y_re, y_im = complex_times(p_re, p_im, real_part, imag_part)
            x_re, x_im = times_conj(y_re, y_im, q_re, q_im)
            return (running + jnp.concatenate([x_re, x_im], axis=1), None)
        running, _ = lax.scan(facet_step, jnp.zeros((tile_width, 2 * tile_width), jnp.float32), facet_ids)
        return running
    predicted = lax.map(predict_tile, (offsets, stations))
    residual_vis = jnp.where(live_mask[:, None, None], observed - predicted, jnp.zeros_like(observed))
    image_scale = 1.0 / (32.0 * tile_width * math.sqrt(tile_total))

    def image_facet(facet_id):

        def tile_step(running, tile_args):
            tile_offset, tile_couple, tile_resid = tile_args
            tab_u, table_vertical = tables(tile_offset[0], tile_offset[1], facet_id, tile_width, facet_cells)
            first_station_gain = screens[facet_id, tile_couple[0]].astype(jnp.float32)
            gain_q = screens[facet_id, tile_couple[1]].astype(jnp.float32)
            p_re, p_im = half_splits(first_station_gain)
            q_re, q_im = half_splits(gain_q)
            r_re, r_im = half_splits(tile_resid)
            z_re, z_im = times_conj(r_re, r_im, p_re, p_im)
            w_re, w_im = complex_times(z_re, z_im, q_re, q_im)
            w_re = w_re.astype(jnp.bfloat16)
            w_im = w_im.astype(jnp.bfloat16)
            stacked = jnp.concatenate([jnp.concatenate([w_re, -w_im], axis=1), jnp.concatenate([w_im, w_re], axis=1)], axis=0)
            q_two = jnp.dot(stacked, table_vertical, preferred_element_type=jnp.float32).astype(jnp.bfloat16)
            return (running + jnp.dot(tab_u.T, q_two, preferred_element_type=jnp.float32), None)
        running, _ = lax.scan(tile_step, jnp.zeros((facet_cells, facet_cells), jnp.float32), (offsets, stations, residual_vis))
        return running * image_scale
    residual_image = lax.map(image_facet, facet_ids)
    return (residual_vis, residual_image)
```

```python
import functools
import math

import jax
import jax.numpy as jnp
from jax import lax
from jax.experimental import pallas as pl
from jax.experimental.pallas import tpu as pltpu
from jax.sharding import PartitionSpec as P

FGRID = 4
F32 = jnp.float32
BF16 = jnp.bfloat16


def cis(k, cells):
    shift = (cells // 4).bit_length() - 1
    turn = (k + cells // 8) >> shift
    x = (k - (turn << shift)).astype(F32) * (2.0 * math.pi / cells)
    y = x * x
    s = x * (1.0 + y * (-1.0 / 6 + y * (1.0 / 120 + y * (-1.0 / 5040 + y * (1.0 / 362880)))))
    c = 1.0 + y * (-0.5 + y * (1.0 / 24 + y * (-1.0 / 720 + y * (1.0 / 40320))))
    odd = (turn & 1) == 1
    cos = jnp.where(odd, s, c)
    sin = jnp.where(odd, c, s)
    cos = jnp.where(((turn + 1) & 2) == 2, -cos, cos)
    sin = jnp.where((turn & 2) == 2, -sin, sin)
    return cos, sin


def kernel(
    dims,
    meta_ref,
    model_ref,
    screens_ref,
    obs_ref,
    image_ref,
    resout_ref,
    meta_land,
    meta_all,
    e2u,
    e1u,
    e1v,
    wv,
    tabu,
    scr_land,
    sbuf,
    s_land,
    sown,
    gbuf,
    cbuf,
    c_land,
    obs_land,
    obsfull,
    livefull,
    res16,
    r_land,
    rall,
    zsend,
    reso,
    z_send,
    z_recv,
    p_send,
    p_recv,
    own_sem,
):
    F, B, T, TD, G, PX, rows, Uc, UB, RPF, nu, per = dims
    N = FGRID * PX
    f = lax.axis_index("facet")
    me = lax.axis_index("bl")
    spd = screens_ref.shape[1]
    UBT = UB * T
    H = G

    barrier = pltpu.get_barrier_semaphore()
    for k in range(1, B):
        pl.semaphore_signal(
            barrier, inc=1, device_id={"bl": lax.rem(me + k, B)},
            device_id_type=pl.DeviceIdType.MESH,
        )
    for k in range(1, F):
        pl.semaphore_signal(
            barrier, inc=1, device_id={"facet": lax.rem(f + k, F)},
            device_id_type=pl.DeviceIdType.MESH,
        )

    def zcopy(stage, k, src, dst):
        return pltpu.make_async_remote_copy(
            src_ref=src, dst_ref=dst, send_sem=z_send.at[stage, k], recv_sem=z_recv.at[stage, k],
            device_id={"bl": lax.rem(me + k, B)}, device_id_type=pl.DeviceIdType.MESH,
        )

    def pcopy(stage, k, src, dst):
        return pltpu.make_async_remote_copy(
            src_ref=src, dst_ref=dst, send_sem=p_send.at[stage, k], recv_sem=p_recv.at[stage, k],
            device_id={"facet": lax.rem(f + k, F)}, device_id_type=pl.DeviceIdType.MESH,
        )

    def scr_rows(s):
        return pl.ds(pl.multiple_of(s * spd, spd), spd)

    corner_x = (f // FGRID) * PX
    corner_y = (f % FGRID) * PX
    pix_u = lax.broadcasted_iota(jnp.int32, (1, rows), 1) + (corner_x + me * rows)
    pix_v = lax.broadcasted_iota(jnp.int32, (1, PX), 1) + corner_y

    pl.semaphore_wait(barrier, B + F - 2)

    meta_copies = [zcopy(0, k, meta_ref, meta_land.at[me]) for k in range(1, B)]
    obs_copies = []
    scr_copies = []
    for k in range(1, B):
        c = lax.rem(me + k, B)
        u0 = c * Uc + (f // per) * nu
        obs_copies.append(zcopy(1, k, obs_ref.at[pl.ds(u0, nu)], obs_land.at[me]))
        scr_copies.append(
            zcopy(2, k, screens_ref.at[pl.ds(c * Uc, Uc)], scr_land.at[:, scr_rows(me)])
        )
    for group in (meta_copies, obs_copies, scr_copies):
        for copy in group:
            copy.start()
    own_copy = pltpu.make_async_copy(
        screens_ref.at[pl.ds(me * Uc, Uc)], scr_land.at[:, scr_rows(me)], own_sem
    )
    own_copy.start()
    meta_land[me] = meta_ref[...]
    obs_land[me] = obs_ref[pl.ds(me * Uc + (f // per) * nu, nu)]

    cells = lax.broadcasted_iota(jnp.int32, (G, 1), 0)
    cu, su = cis(cells * pix_u, N)
    e2u[0] = cu
    e2u[1] = su
    for j in range(0, PX, 256):
        cv, sv = cis(cells * pix_v[:, j : j + 256], N)
        wv[:H, j : j + 256] = cv.astype(BF16)
        wv[H:, j : j + 256] = sv.astype(BF16)

    for copy in meta_copies:
        copy.wait()
    for b in range(B):
        meta_all[b * TD : (b + 1) * TD, :] = meta_land[b, :TD, :]
    ou = meta_all[:, 0:1]
    ov = meta_all[:, 1:2]
    c1, s1 = cis(ou * pix_u, N)
    e1u[0] = c1
    e1u[1] = s1
    for j in range(0, PX, 256):
        c1, s1 = cis(ov * pix_v[:, j : j + 256], N)
        e1v[0, :, j : j + 256] = c1
        e1v[1, :, j : j + 256] = s1

    lane = lax.broadcasted_iota(jnp.int32, (1, 2 * G), 1)
    left = lane < G
    sgn = jnp.where(left, 1.0, -1.0).astype(F32)

    def swap(x):
        return pltpu.roll(x, G, 1)

    nchunk = Uc // UB

    def predict(c, i):
        ci = c * nchunk + i
        for j in range(UB):
            u = c * Uc + i * UB + j
            e2c = e2u[0, pl.ds(u, 1), :]
            e2s = e2u[1, pl.ds(u, 1), :]
            a_c = e1u[0]
            a_s = e1u[1]
            tabu[ci, j * T : (j + 1) * T, :] = (a_c * e2c - a_s * e2s).astype(BF16)
            tabu[ci, UBT + j * T : UBT + (j + 1) * T, :] = (-(a_s * e2c + a_c * e2s)).astype(BF16)
        up = jnp.dot(tabu[ci], model_ref[...], preferred_element_type=F32)
        tops, bots = [], []
        for j in range(UB):
            uc = up[j * T : (j + 1) * T]
            us = up[UBT + j * T : UBT + (j + 1) * T]
            tops.append((uc * e1v[0] + us * e1v[1]).astype(BF16))
            bots.append((us * e1v[0] - uc * e1v[1]).astype(BF16))
        both = jnp.concatenate(tops + bots, axis=0)
        b = lax.dot_general(
            both, wv[...], (((1,), (1,)), ((), ())), preferred_element_type=F32
        )
        return b[:UBT] * sgn + swap(b[UBT:])

    s_copies = []
    for k in range(1, B):
        c = lax.rem(me + k, B)

        def body(i, carry, c=c):
            rows_i = pl.ds(pl.multiple_of(i * UBT, UBT), UBT)
            sbuf[c, rows_i, :] = predict(c, i).astype(BF16)
            return carry

        lax.fori_loop(0, nchunk, body, 0)
        copy = zcopy(3, k, sbuf.at[c], s_land.at[me])
        copy.start()
        s_copies.append(copy)

    def body_own(i, carry):
        rows_i = pl.ds(pl.multiple_of(i * UBT, UBT), UBT)
        sown[rows_i, :] = predict(me, i)
        return carry

    lax.fori_loop(0, nchunk, body_own, 0)

    for copy in obs_copies:
        copy.wait()
    for j in range(nu):
        for b in range(B):
            obsfull[j * T + b * TD : j * T + (b + 1) * TD, :] = obs_land[b, j]
        livefull[j * T : (j + 1) * T, :] = jnp.broadcast_to(
            meta_all[:, 4:5].astype(F32), (T, 2 * G)
        )

    own_copy.wait()
    for copy in scr_copies:
        copy.wait()
    stations = lax.broadcasted_iota(jnp.int32, (1, B * spd), 1)
    pick = jnp.concatenate([meta_all[:, 2:3], meta_all[:, 3:4]], axis=0) == stations
    pick = jnp.where(pick, 1.0, 0.0).astype(BF16)

    def gains(u, carry):
        both = jnp.dot(pick, scr_land[u], preferred_element_type=F32)
        p = both[:T]
        q = both[T:]
        qsw = swap(q)
        g = p * jnp.where(left, q, qsw) + swap(p) * jnp.where(left, qsw, -q)
        gbuf[pl.ds(pl.multiple_of(u * T, T), T), :] = g
        return carry

    lax.fori_loop(0, Uc, gains, 0)

    for copy in s_copies:
        copy.wait()

    def contribution(u, carry):
        r = pl.ds(pl.multiple_of(u * T, T), T)
        s = sown[r, :]
        for k in range(1, B):
            s = s + s_land[lax.rem(me + k, B), r, :].astype(F32)
        g = gbuf[r, :]
        gsw = swap(g)
        out = s * jnp.where(left, g, gsw) + swap(s) * jnp.where(left, -gsw, g)
        cbuf[r, :] = out.astype(BF16)
        return carry

    lax.fori_loop(0, Uc, contribution, 0)

    def piece(i):
        return pl.ds(pl.multiple_of(i * RPF, RPF), RPF)

    c_copies = [
        pcopy(0, k, cbuf.at[piece(lax.rem(f + k, F))], c_land.at[f]) for k in range(1, F)
    ]
    for copy in c_copies:
        copy.start()
    total = cbuf[piece(f), :].astype(F32)
    for copy in c_copies:
        copy.wait()
    for k in range(1, F):
        total = total + c_land[lax.rem(f + k, F)].astype(F32)
    span = pl.ds(pl.multiple_of((f % per) * RPF, RPF), RPF)
    res = jnp.where(livefull[span, :] > 0.5, obsfull[span, :] - total, 0.0)
    r_land[piece(f), :] = res.astype(BF16)
    res16[...] = res.astype(BF16)
    r_copies = [pcopy(1, k, res16, r_land.at[piece(f)]) for k in range(1, F)]
    for copy in r_copies:
        copy.start()
    if per > 1:
        obsfull[...] = jnp.zeros_like(obsfull)
    obsfull[span, :] = res
    for j in range(nu):
        for b in range(B):
            zsend[b, j] = obsfull[j * T + b * TD : j * T + (b + 1) * TD, :]
    reso[f, me] = zsend[me]
    for copy in r_copies:
        copy.wait()

    def weigh(u, carry):
        r = pl.ds(pl.multiple_of(u * T, T), T)
        x = r_land[r, :].astype(F32)
        g = gbuf[r, :]
        gsw = swap(g)
        out = x * jnp.where(left, g, gsw) + swap(x) * jnp.where(left, gsw, -g)
        rall[me, r, :] = out.astype(BF16)
        return carry

    lax.fori_loop(0, Uc, weigh, 0)
    w_copies = [zcopy(4, k, rall.at[me], rall.at[me]) for k in range(1, B)]
    for copy in w_copies:
        copy.start()
    z_copies = [
        zcopy(5, k, zsend.at[lax.rem(me + k, B)], reso.at[f, me]) for k in range(1, B)
    ]
    for copy in z_copies:
        copy.start()

    image_ref[...] = jnp.zeros_like(image_ref)

    def image(src):
        def body(i, carry):
            ci = src * nchunk + i
            r = rall[src, pl.ds(pl.multiple_of(i * UBT, UBT), UBT), :].astype(F32)
            both = jnp.concatenate([(r * sgn).astype(BF16), swap(r).astype(BF16)], axis=0)
            prod = jnp.dot(both, wv[...], preferred_element_type=F32)
            tops, bots = [], []
            for j in range(UB):
                pc = prod[j * T : (j + 1) * T]
                ps = prod[UBT + j * T : UBT + (j + 1) * T]
                tops.append((pc * e1v[0] - ps * e1v[1]).astype(BF16))
                bots.append((ps * e1v[0] + pc * e1v[1]).astype(BF16))
            q2 = jnp.concatenate(tops + bots, axis=0)
            image_ref[...] += lax.dot_general(
                tabu[ci], q2, (((0,), (0,)), ((), ())), preferred_element_type=F32
            )
            return carry

        lax.fori_loop(0, nchunk, body, 0)

    image(me)
    for copy in z_copies:
        copy.wait()
    o_copies = [pcopy(2, k, reso.at[f], reso.at[f]) for k in range(1, F)]
    for copy in o_copies:
        copy.start()
    for k in range(1, B):
        w_copies[k - 1].wait()
        image(lax.rem(me + B - k, B))
    image_ref[...] = image_ref[...] * (1.0 / (32.0 * G * math.sqrt(T)))
    for copy in o_copies:
        copy.wait()
    resout_ref[...] = reso[...]


def per_device(F, B, facet_model, screens, observed, offsets, stations, counts):
    TD, G = observed.shape[0], observed.shape[1]
    PX = facet_model.shape[2]
    rows = facet_model.shape[1]
    spd = screens.shape[1]
    T = TD * B
    Uc = G // B
    UB = max(1, min(Uc, 192 // T))
    RPF = Uc * T // F
    nu = max(1, RPF // T)
    per = max(1, T // RPF)
    dims = (F, B, T, TD, G, PX, rows, Uc, UB, RPF, nu, per)
    tdp = -(-TD // 8) * 8
    live = (jnp.arange(TD, dtype=jnp.int32) < counts[0]).astype(jnp.int32)[:, None]
    meta = jnp.concatenate([offsets, stations, live], axis=1)
    meta = jnp.pad(meta, ((0, tdp - TD), (0, 128 - meta.shape[1])))
    screens_t = jnp.transpose(screens[0], (1, 0, 2))
    obs_t = jnp.transpose(observed, (1, 0, 2))
    W = 2 * G
    vmem = pl.BlockSpec(memory_space=pltpu.VMEM)
    image, res = pl.pallas_call(
        functools.partial(kernel, dims),
        out_shape=(
            jax.ShapeDtypeStruct((rows, PX), F32),
            jax.ShapeDtypeStruct((F, B, nu, TD, W), F32),
        ),
        in_specs=[vmem] * 4,
        out_specs=(vmem, vmem),
        scratch_shapes=[
            pltpu.VMEM((B, tdp, 128), jnp.int32),
            pltpu.VMEM((T, 128), jnp.int32),
            pltpu.VMEM((2, G, rows), F32),
            pltpu.VMEM((2, T, rows), F32),
            pltpu.VMEM((2, T, PX), F32),
            pltpu.VMEM((W, PX), BF16),
            pltpu.VMEM((G // UB, 2 * UB * T, rows), BF16),
            pltpu.VMEM((Uc, B * spd, W), BF16),
            pltpu.VMEM((B, Uc * T, W), BF16),
            pltpu.VMEM((B, Uc * T, W), BF16),
            pltpu.VMEM((Uc * T, W), F32),
            pltpu.VMEM((Uc * T, W), F32),
            pltpu.VMEM((Uc * T, W), BF16),
            pltpu.VMEM((F, RPF, W), BF16),
            pltpu.VMEM((B, nu, TD, W), F32),
            pltpu.VMEM((nu * T, W), F32),
            pltpu.VMEM((nu * T, W), F32),
            pltpu.VMEM((RPF, W), BF16),
            pltpu.VMEM((Uc * T, W), BF16),
            pltpu.VMEM((B, Uc * T, W), BF16),
            pltpu.VMEM((B, nu, TD, W), F32),
            pltpu.VMEM((F, B, nu, TD, W), F32),
            pltpu.SemaphoreType.DMA((6, B)),
            pltpu.SemaphoreType.DMA((6, B)),
            pltpu.SemaphoreType.DMA((3, F)),
            pltpu.SemaphoreType.DMA((3, F)),
            pltpu.SemaphoreType.DMA,
        ],
        compiler_params=pltpu.CompilerParams(
            collective_id=0, has_side_effects=True, vmem_limit_bytes=56 * 1024 * 1024
        ),
    )(meta, facet_model[0], screens_t, obs_t)
    group = lax.axis_index("bl") * TD // RPF if per > 1 else 0
    res = res.reshape(F // per, per, B, nu, TD, W)
    res = lax.dynamic_index_in_dim(res, group, axis=1, keepdims=False)
    res = jnp.transpose(res, (3, 1, 0, 2, 4)).reshape(TD, G, W)
    return (res, image[None])


def solution(mesh):
    in_specs = (
        P("facet", "bl", None),
        P("facet", "bl", None, None),
        P("bl", None, None),
        P("bl", None),
        P("bl", None),
        P("bl"),
    )
    out_specs = (P("bl", None, None), P("facet", "bl", None))
    return jax.shard_map(
        functools.partial(per_device, mesh.shape["facet"], mesh.shape["bl"]),
        mesh=mesh, in_specs=in_specs, out_specs=out_specs, check_vma=False,
    )
```

```python
import functools
import math

import jax
import jax.numpy as jnp
from jax import lax
from jax.experimental import pallas as pl
from jax.experimental.pallas import tpu as pltpu
from jax.sharding import PartitionSpec as P

FGRID = 4
F32 = jnp.float32
BF16 = jnp.bfloat16


def cis(k, cells):
    shift = (cells // 4).bit_length() - 1
    turn = (k + cells // 8) >> shift
    x = (k - (turn << shift)).astype(F32) * (2.0 * math.pi / cells)
    y = x * x
    s = x * (1.0 + y * (-1.0 / 6 + y * (1.0 / 120 + y * (-1.0 / 5040 + y * (1.0 / 362880)))))
    c = 1.0 + y * (-0.5 + y * (1.0 / 24 + y * (-1.0 / 720 + y * (1.0 / 40320))))
    odd = (turn & 1) == 1
    cos = jnp.where(odd, s, c)
    sin = jnp.where(odd, c, s)
    cos = jnp.where(((turn + 1) & 2) == 2, -cos, cos)
    sin = jnp.where((turn & 2) == 2, -sin, sin)
    return cos, sin


def kernel(
    dims,
    offsets_ref,
    stations_ref,
    counts_ref,
    model_ref,
    screens_ref,
    obs_ref,
    image_ref,
    pred_ref,
    meta_ref,
    meta_land,
    osend,
    meta_all,
    e2u,
    e1u,
    e1v,
    wv,
    tabu,
    scr_land,
    sbuf,
    s_land,
    sown,
    gbuf,
    cbuf,
    c_land,
    obs_land,
    obsfull,
    livefull,
    res16,
    r_land,
    rall,
    zsend,
    reso,
    z_send,
    z_recv,
    p_send,
    p_recv,
    w_send,
    w_recv,
    own_sem,
):
    F, B, T, TD, G, PX, rows, Uc, UB, RPF, nu, per = dims
    N = FGRID * PX
    f = lax.axis_index("facet")
    me = lax.axis_index("bl")
    spd = screens_ref.shape[1]
    UBT = UB * T
    H = G

    barrier = pltpu.get_barrier_semaphore()
    for k in range(1, B):
        pl.semaphore_signal(
            barrier, inc=1, device_id={"bl": lax.rem(me + k, B)},
            device_id_type=pl.DeviceIdType.MESH,
        )
    for k in range(1, F):
        pl.semaphore_signal(
            barrier, inc=1, device_id={"facet": lax.rem(f + k, F)},
            device_id_type=pl.DeviceIdType.MESH,
        )

    def zcopy(stage, k, src, dst):
        return pltpu.make_async_remote_copy(
            src_ref=src, dst_ref=dst, send_sem=z_send.at[stage, k], recv_sem=z_recv.at[stage, k],
            device_id={"bl": lax.rem(me + k, B)}, device_id_type=pl.DeviceIdType.MESH,
        )

    def pcopy(stage, k, src, dst):
        return pltpu.make_async_remote_copy(
            src_ref=src, dst_ref=dst, send_sem=p_send.at[stage, k], recv_sem=p_recv.at[stage, k],
            device_id={"facet": lax.rem(f + k, F)}, device_id_type=pl.DeviceIdType.MESH,
        )

    def scr_rows(s):
        return pl.ds(pl.multiple_of(s * spd, spd), spd)

    corner_x = (f // FGRID) * PX
    corner_y = (f % FGRID) * PX
    pix_u = lax.broadcasted_iota(jnp.int32, (1, rows), 1) + (corner_x + me * rows)
    pix_v = lax.broadcasted_iota(jnp.int32, (1, PX), 1) + corner_y

    row = lax.broadcasted_iota(jnp.int32, meta_ref.shape, 0)
    col = lax.broadcasted_iota(jnp.int32, meta_ref.shape, 1)
    meta = jnp.where((col == 4) & (row < counts_ref[0]), 1, 0)
    for t in range(TD):
        for j in range(2):
            meta = jnp.where((row == t) & (col == j), offsets_ref[t, j], meta)
            meta = jnp.where((row == t) & (col == j + 2), stations_ref[t, j], meta)
    meta_ref[...] = meta
    for k in range(B):
        c = lax.rem(me + k, B)
        for j in range(nu):
            u = c * Uc + (f // per) * nu + j
            osend[c, j] = obs_ref[pl.ds(u, TD, stride=G), :]

    pl.semaphore_wait(barrier, B + F - 2)

    meta_copies = [zcopy(0, k, meta_ref, meta_land.at[me]) for k in range(1, B)]
    obs_copies = []
    scr_copies = []
    for k in range(1, B):
        c = lax.rem(me + k, B)
        obs_copies.append(zcopy(1, k, osend.at[c], obs_land.at[me]))
        scr_copies.append(
            zcopy(2, k, screens_ref.at[pl.ds(c * Uc, Uc)], scr_land.at[:, scr_rows(me)])
        )
    for group in (meta_copies, obs_copies, scr_copies):
        for copy in group:
            copy.start()
    own_copy = pltpu.make_async_copy(
        screens_ref.at[pl.ds(me * Uc, Uc)], scr_land.at[:, scr_rows(me)], own_sem
    )
    own_copy.start()
    meta_land[me] = meta_ref[...]
    obs_land[me] = osend[me]

    cells = lax.broadcasted_iota(jnp.int32, (G, 1), 0)
    cu, su = cis(cells * pix_u, N)
    e2u[0] = cu
    e2u[1] = su
    for j in range(0, PX, 256):
        cv, sv = cis(cells * pix_v[:, j : j + 256], N)
        wv[:H, j : j + 256] = cv.astype(BF16)
        wv[H:, j : j + 256] = sv.astype(BF16)

    for copy in meta_copies:
        copy.wait()
    for b in range(B):
        meta_all[b * TD : (b + 1) * TD, :] = meta_land[b, :TD, :]
    ou = meta_all[:, 0:1]
    ov = meta_all[:, 1:2]
    c1, s1 = cis(ou * pix_u, N)
    e1u[0] = c1
    e1u[1] = s1
    for j in range(0, PX, 256):
        c1, s1 = cis(ov * pix_v[:, j : j + 256], N)
        e1v[0, :, j : j + 256] = c1
        e1v[1, :, j : j + 256] = s1

    lane = lax.broadcasted_iota(jnp.int32, (1, 2 * G), 1)
    left = lane < G
    sgn = jnp.where(left, 1.0, -1.0).astype(F32)

    def swap(x):
        return pltpu.roll(x, G, 1)

    nchunk = Uc // UB

    def predict(c, i):
        ci = c * nchunk + i
        for j in range(UB):
            u = c * Uc + i * UB + j
            e2c = e2u[0, pl.ds(u, 1), :]
            e2s = e2u[1, pl.ds(u, 1), :]
            a_c = e1u[0]
            a_s = e1u[1]
            tabu[ci, j * T : (j + 1) * T, :] = (a_c * e2c - a_s * e2s).astype(BF16)
            tabu[ci, UBT + j * T : UBT + (j + 1) * T, :] = (-(a_s * e2c + a_c * e2s)).astype(BF16)
        up = jnp.dot(tabu[ci], model_ref[...], preferred_element_type=F32)
        tops, bots = [], []
        for j in range(UB):
            uc = up[j * T : (j + 1) * T]
            us = up[UBT + j * T : UBT + (j + 1) * T]
            tops.append((uc * e1v[0] + us * e1v[1]).astype(BF16))
            bots.append((us * e1v[0] - uc * e1v[1]).astype(BF16))
        both = jnp.concatenate(tops + bots, axis=0)
        b = lax.dot_general(
            both, wv[...], (((1,), (1,)), ((), ())), preferred_element_type=F32
        )
        return b[:UBT] * sgn + swap(b[UBT:])

    s_copies = []
    for k in range(1, B):
        c = lax.rem(me + k, B)

        def body(i, carry, c=c):
            rows_i = pl.ds(pl.multiple_of(i * UBT, UBT), UBT)
            sbuf[c, rows_i, :] = predict(c, i).astype(BF16)
            return carry

        lax.fori_loop(0, nchunk, body, 0)
        copy = zcopy(3, k, sbuf.at[c], s_land.at[me])
        copy.start()
        s_copies.append(copy)

    def body_own(i, carry):
        rows_i = pl.ds(pl.multiple_of(i * UBT, UBT), UBT)
        sown[rows_i, :] = predict(me, i)
        return carry

    lax.fori_loop(0, nchunk, body_own, 0)

    for copy in obs_copies:
        copy.wait()
    for j in range(nu):
        for b in range(B):
            obsfull[j * T + b * TD : j * T + (b + 1) * TD, :] = obs_land[b, j]
        livefull[j * T : (j + 1) * T, :] = jnp.broadcast_to(
            meta_all[:, 4:5].astype(F32), (T, 2 * G)
        )

    own_copy.wait()
    for copy in scr_copies:
        copy.wait()
    stations = lax.broadcasted_iota(jnp.int32, (1, B * spd), 1)
    pick = jnp.concatenate([meta_all[:, 2:3], meta_all[:, 3:4]], axis=0) == stations
    pick = jnp.where(pick, 1.0, 0.0).astype(BF16)

    def gains(u, carry):
        both = jnp.dot(pick, scr_land[u], preferred_element_type=F32)
        p = both[:T]
        q = both[T:]
        qsw = swap(q)
        g = p * jnp.where(left, q, qsw) + swap(p) * jnp.where(left, qsw, -q)
        gbuf[pl.ds(pl.multiple_of(u * T, T), T), :] = g
        return carry

    lax.fori_loop(0, Uc, gains, 0)

    for copy in s_copies:
        copy.wait()

    def contribution(u, carry):
        r = pl.ds(pl.multiple_of(u * T, T), T)
        s = sown[r, :]
        for k in range(1, B):
            s = s + s_land[lax.rem(me + k, B), r, :].astype(F32)
        g = gbuf[r, :]
        gsw = swap(g)
        out = s * jnp.where(left, g, gsw) + swap(s) * jnp.where(left, -gsw, g)
        cbuf[r, :] = out.astype(BF16)
        return carry

    lax.fori_loop(0, Uc, contribution, 0)

    def piece(i):
        return pl.ds(pl.multiple_of(i * RPF, RPF), RPF)

    c_copies = [
        pcopy(0, k, cbuf.at[piece(lax.rem(f + k, F))], c_land.at[f]) for k in range(1, F)
    ]
    for copy in c_copies:
        copy.start()
    total = cbuf[piece(f), :].astype(F32)
    for copy in c_copies:
        copy.wait()
    for k in range(1, F):
        total = total + c_land[lax.rem(f + k, F)].astype(F32)
    span = pl.ds(pl.multiple_of((f % per) * RPF, RPF), RPF)
    res = jnp.where(livefull[span, :] > 0.5, obsfull[span, :] - total, 0.0)
    r_land[piece(f), :] = res.astype(BF16)
    res16[...] = res.astype(BF16)
    r_copies = [pcopy(1, k, res16, r_land.at[piece(f)]) for k in range(1, F)]
    for copy in r_copies:
        copy.start()
    if per > 1:
        obsfull[...] = jnp.zeros_like(obsfull)
    obsfull[span, :] = total
    for j in range(nu):
        for b in range(B):
            zsend[b, j] = obsfull[j * T + b * TD : j * T + (b + 1) * TD, :]
    reso[f, me] = zsend[me]
    for copy in r_copies:
        copy.wait()

    def weigh(u, carry):
        r = pl.ds(pl.multiple_of(u * T, T), T)
        x = r_land[r, :].astype(F32)
        g = gbuf[r, :]
        gsw = swap(g)
        out = x * jnp.where(left, g, gsw) + swap(x) * jnp.where(left, gsw, -g)
        rall[me, r, :] = out.astype(BF16)
        return carry

    lax.fori_loop(0, Uc, weigh, 0)

    def right(n):
        block = jnp.maximum(me - n, 0)
        return pltpu.make_async_remote_copy(
            src_ref=rall.at[block], dst_ref=rall.at[block],
            send_sem=w_send.at[0, n], recv_sem=w_recv.at[0, n],
            device_id={"bl": lax.rem(me + 1, B)}, device_id_type=pl.DeviceIdType.MESH,
        )

    def left_(n):
        block = jnp.minimum(me + n, B - 1)
        return pltpu.make_async_remote_copy(
            src_ref=rall.at[block], dst_ref=rall.at[block],
            send_sem=w_send.at[1, n], recv_sem=w_recv.at[1, n],
            device_id={"bl": lax.rem(me + B - 1, B)}, device_id_type=pl.DeviceIdType.MESH,
        )

    def sends_right(n):
        return (me - n >= 0) & (me + 1 < B)

    def sends_left(n):
        return (me + n < B) & (me >= 1)

    pl.when(sends_right(0))(lambda: right(0).start())
    pl.when(sends_left(0))(lambda: left_(0).start())
    z_copies = [
        zcopy(5, k, zsend.at[lax.rem(me + k, B)], reso.at[f, me]) for k in range(1, B)
    ]
    for copy in z_copies:
        copy.start()

    image_ref[...] = jnp.zeros_like(image_ref)

    def image(src):
        def body(i, carry):
            ci = src * nchunk + i
            r = rall[src, pl.ds(pl.multiple_of(i * UBT, UBT), UBT), :].astype(F32)
            both = jnp.concatenate([(r * sgn).astype(BF16), swap(r).astype(BF16)], axis=0)
            prod = jnp.dot(both, wv[...], preferred_element_type=F32)
            tops, bots = [], []
            for j in range(UB):
                pc = prod[j * T : (j + 1) * T]
                ps = prod[UBT + j * T : UBT + (j + 1) * T]
                tops.append((pc * e1v[0] - ps * e1v[1]).astype(BF16))
                bots.append((ps * e1v[0] + pc * e1v[1]).astype(BF16))
            q2 = jnp.concatenate(tops + bots, axis=0)
            image_ref[...] += lax.dot_general(
                tabu[ci], q2, (((0,), (0,)), ((), ())), preferred_element_type=F32
            )
            return carry

        lax.fori_loop(0, nchunk, body, 0)

    image(me)
    for copy in z_copies:
        copy.wait()
    o_copies = [pcopy(2, k, reso.at[f], reso.at[f]) for k in range(1, F)]
    for copy in o_copies:
        copy.start()
    for n in range(B - 1):
        pl.when(me - 1 - n >= 0)(lambda n=n: right(n).wait_recv())
        if n + 1 < B - 1:
            pl.when(sends_right(n + 1))(lambda n=n: right(n + 1).start())
        pl.when(me + 1 + n < B)(lambda n=n: left_(n).wait_recv())
        if n + 1 < B - 1:
            pl.when(sends_left(n + 1))(lambda n=n: left_(n + 1).start())

        def arrived(side, carry, n=n):
            src = jnp.where(side == 0, me - 1 - n, me + 1 + n)
            pl.when((src >= 0) & (src < B))(lambda: image(src))
            return carry

        lax.fori_loop(0, 2, arrived, 0)
    for n in range(B - 1):
        pl.when(sends_right(n))(lambda n=n: right(n).wait_send())
        pl.when(sends_left(n))(lambda n=n: left_(n).wait_send())
    for copy in o_copies:
        copy.wait()
    group = (me * TD) // RPF if per > 1 else 0
    for g in range(F // per):
        for c in range(B):
            for j in range(nu):
                u = c * Uc + g * nu + j
                pred_ref[pl.ds(u, TD, stride=G), :] = reso[g * per + group, c, j]


def per_device(F, B, facet_model, screens, observed, offsets, stations, counts):
    TD, G = observed.shape[0], observed.shape[1]
    PX = facet_model.shape[2]
    rows = facet_model.shape[1]
    spd = screens.shape[1]
    T = TD * B
    Uc = G // B
    UB = max(1, min(Uc, 192 // T))
    RPF = Uc * T // F
    nu = max(1, RPF // T)
    per = max(1, T // RPF)
    dims = (F, B, T, TD, G, PX, rows, Uc, UB, RPF, nu, per)
    tdp = -(-TD // 8) * 8
    screens_t = jnp.transpose(screens[0], (1, 0, 2))
    W = 2 * G
    vmem = pl.BlockSpec(memory_space=pltpu.VMEM)
    smem = pl.BlockSpec(memory_space=pltpu.SMEM)
    image, predicted = pl.pallas_call(
        functools.partial(kernel, dims),
        out_shape=(
            jax.ShapeDtypeStruct((rows, PX), F32),
            jax.ShapeDtypeStruct((TD * G, W), F32),
        ),
        in_specs=[smem] * 3 + [vmem] * 3,
        out_specs=(vmem, vmem),
        scratch_shapes=[
            pltpu.VMEM((tdp, 128), jnp.int32),
            pltpu.VMEM((B, tdp, 128), jnp.int32),
            pltpu.VMEM((B, nu, TD, W), F32),
            pltpu.VMEM((T, 128), jnp.int32),
            pltpu.VMEM((2, G, rows), F32),
            pltpu.VMEM((2, T, rows), F32),
            pltpu.VMEM((2, T, PX), F32),
            pltpu.VMEM((W, PX), BF16),
            pltpu.VMEM((G // UB, 2 * UB * T, rows), BF16),
            pltpu.VMEM((Uc, B * spd, W), BF16),
            pltpu.VMEM((B, Uc * T, W), BF16),
            pltpu.VMEM((B, Uc * T, W), BF16),
            pltpu.VMEM((Uc * T, W), F32),
            pltpu.VMEM((Uc * T, W), F32),
            pltpu.VMEM((Uc * T, W), BF16),
            pltpu.VMEM((F, RPF, W), BF16),
            pltpu.VMEM((B, nu, TD, W), F32),
            pltpu.VMEM((nu * T, W), F32),
            pltpu.VMEM((nu * T, W), F32),
            pltpu.VMEM((RPF, W), BF16),
            pltpu.VMEM((Uc * T, W), BF16),
            pltpu.VMEM((B, Uc * T, W), BF16),
            pltpu.VMEM((B, nu, TD, W), F32),
            pltpu.VMEM((F, B, nu, TD, W), F32),
            pltpu.SemaphoreType.DMA((6, B)),
            pltpu.SemaphoreType.DMA((6, B)),
            pltpu.SemaphoreType.DMA((3, F)),
            pltpu.SemaphoreType.DMA((3, F)),
            pltpu.SemaphoreType.DMA((2, B)),
            pltpu.SemaphoreType.DMA((2, B)),
            pltpu.SemaphoreType.DMA,
        ],
        compiler_params=pltpu.CompilerParams(
            collective_id=0, has_side_effects=True, vmem_limit_bytes=56 * 1024 * 1024
        ),
    )(offsets, stations, counts, facet_model[0], screens_t, observed.reshape(TD * G, W))
    live = (jnp.arange(TD, dtype=jnp.int32) < counts[0])[:, None, None]
    residual = jnp.where(live, observed - predicted.reshape(TD, G, W), 0.0)
    return (residual, image[None] * (1.0 / (32.0 * G * math.sqrt(T))))


def solution(mesh):
    in_specs = (
        P("facet", "bl", None),
        P("facet", "bl", None, None),
        P("bl", None, None),
        P("bl", None),
        P("bl", None),
        P("bl"),
    )
    out_specs = (P("bl", None, None), P("facet", "bl", None))
    return jax.shard_map(
        functools.partial(per_device, mesh.shape["facet"], mesh.shape["bl"]),
        mesh=mesh, in_specs=in_specs, out_specs=out_specs, check_vma=False,
    )
```

```python
import functools
import math

import jax
import jax.numpy as jnp
from jax import lax
from jax.experimental import pallas as pl
from jax.experimental.pallas import tpu as pltpu
from jax.sharding import PartitionSpec as P

FGRID = 4
F32 = jnp.float32
BF16 = jnp.bfloat16


def cis(k, cells):
    shift = (cells // 4).bit_length() - 1
    turn = (k + cells // 8) >> shift
    x = (k - (turn << shift)).astype(F32) * (2.0 * math.pi / cells)
    y = x * x
    s = x * (1.0 + y * (-1.0 / 6 + y * (1.0 / 120 + y * (-1.0 / 5040 + y * (1.0 / 362880)))))
    c = 1.0 + y * (-0.5 + y * (1.0 / 24 + y * (-1.0 / 720 + y * (1.0 / 40320))))
    odd = (turn & 1) == 1
    cos = jnp.where(odd, s, c)
    sin = jnp.where(odd, c, s)
    cos = jnp.where(((turn + 1) & 2) == 2, -cos, cos)
    sin = jnp.where((turn & 2) == 2, -sin, sin)
    return cos, sin


def kernel(
    dims,
    offsets_ref,
    stations_ref,
    counts_ref,
    model_ref,
    screens_ref,
    obs_ref,
    image_ref,
    pred_ref,
    meta_ref,
    meta_land,
    osend,
    meta_all,
    e2u,
    e1u,
    e1v,
    wv,
    tabu,
    scr_raw,
    scr_land,
    sbuf,
    s_land,
    sown,
    gbuf,
    cbuf,
    c_land,
    obs_land,
    obsfull,
    livefull,
    res16,
    r_land,
    rall,
    zsend,
    reso,
    z_send,
    z_recv,
    p_send,
    p_recv,
    w_send,
    w_recv,
    s_send,
    s_recv,
    own_sem,
):
    F, B, T, TD, G, PX, rows, Uc, UB, RPF, nu, per = dims
    N = FGRID * PX
    f = lax.axis_index("facet")
    me = lax.axis_index("bl")
    raw = Uc % 16 == 0
    spd = screens_ref.shape[0 if raw else 1]
    UBT = UB * T
    H = G

    barrier = pltpu.get_barrier_semaphore()
    for k in range(1, B):
        pl.semaphore_signal(
            barrier, inc=1, device_id={"bl": lax.rem(me + k, B)},
            device_id_type=pl.DeviceIdType.MESH,
        )
    for k in range(1, F):
        pl.semaphore_signal(
            barrier, inc=1, device_id={"facet": lax.rem(f + k, F)},
            device_id_type=pl.DeviceIdType.MESH,
        )

    def zcopy(stage, k, src, dst):
        return pltpu.make_async_remote_copy(
            src_ref=src, dst_ref=dst, send_sem=z_send.at[stage, k], recv_sem=z_recv.at[stage, k],
            device_id={"bl": lax.rem(me + k, B)}, device_id_type=pl.DeviceIdType.MESH,
        )

    def pcopy(stage, k, src, dst):
        return pltpu.make_async_remote_copy(
            src_ref=src, dst_ref=dst, send_sem=p_send.at[stage, k], recv_sem=p_recv.at[stage, k],
            device_id={"facet": lax.rem(f + k, F)}, device_id_type=pl.DeviceIdType.MESH,
        )

    def scr_rows(s):
        return pl.ds(pl.multiple_of(s * spd, spd), spd)

    corner_x = (f // FGRID) * PX
    corner_y = (f % FGRID) * PX
    pix_u = lax.broadcasted_iota(jnp.int32, (1, rows), 1) + (corner_x + me * rows)
    pix_v = lax.broadcasted_iota(jnp.int32, (1, PX), 1) + corner_y

    row = lax.broadcasted_iota(jnp.int32, meta_ref.shape, 0)
    col = lax.broadcasted_iota(jnp.int32, meta_ref.shape, 1)
    meta = jnp.where((col == 4) & (row < counts_ref[0]), 1, 0)
    for t in range(TD):
        for j in range(2):
            meta = jnp.where((row == t) & (col == j), offsets_ref[j, t], meta)
            meta = jnp.where((row == t) & (col == j + 2), stations_ref[j, t], meta)
    meta_ref[...] = meta
    for k in range(B):
        c = lax.rem(me + k, B)
        for j in range(nu):
            u = c * Uc + (f // per) * nu + j
            osend[c, j] = obs_ref[pl.ds(u, TD, stride=G), :]

    pl.semaphore_wait(barrier, B + F - 2)

    meta_copies = [zcopy(0, k, meta_ref, meta_land.at[me]) for k in range(1, B)]
    obs_copies = []
    scr_copies = []
    for k in range(1, B):
        c = lax.rem(me + k, B)
        obs_copies.append(zcopy(1, k, osend.at[c], obs_land.at[me]))
        if raw:
            rows_c = pl.ds(pl.multiple_of(c * Uc, Uc), Uc)
            scr_copies.append(zcopy(2, k, screens_ref.at[:, rows_c], scr_raw.at[me]))
        else:
            scr_copies.append(
                zcopy(2, k, screens_ref.at[pl.ds(c * Uc, Uc)], scr_land.at[:, scr_rows(me)])
            )
    for group in (meta_copies, obs_copies, scr_copies[0::2]):
        for copy in group:
            copy.start()
    if raw:
        own_copy = pltpu.make_async_copy(
            screens_ref.at[:, pl.ds(pl.multiple_of(me * Uc, Uc), Uc)], scr_raw.at[me], own_sem
        )
    else:
        own_copy = pltpu.make_async_copy(
            screens_ref.at[pl.ds(me * Uc, Uc)], scr_land.at[:, scr_rows(me)], own_sem
        )
    own_copy.start()
    meta_land[me] = meta_ref[...]
    obs_land[me] = osend[me]

    cells = lax.broadcasted_iota(jnp.int32, (G, 1), 0)
    cu, su = cis(cells * pix_u, N)
    e2u[0] = cu
    e2u[1] = su
    for j in range(0, PX, 256):
        cv, sv = cis(cells * pix_v[:, j : j + 256], N)
        wv[:H, j : j + 256] = cv.astype(BF16)
        wv[H:, j : j + 256] = sv.astype(BF16)

    for copy in meta_copies:
        copy.wait()
    for b in range(B):
        meta_all[b * TD : (b + 1) * TD, :] = meta_land[b, :TD, :]
    ou = meta_all[:, 0:1]
    ov = meta_all[:, 1:2]
    c1, s1 = cis(ou * pix_u, N)
    e1u[0] = c1
    e1u[1] = s1
    for j in range(0, PX, 256):
        c1, s1 = cis(ov * pix_v[:, j : j + 256], N)
        e1v[0, :, j : j + 256] = c1
        e1v[1, :, j : j + 256] = s1

    lane = lax.broadcasted_iota(jnp.int32, (1, 2 * G), 1)
    left = lane < G
    sgn = jnp.where(left, 1.0, -1.0).astype(F32)

    def swap(x):
        return pltpu.roll(x, G, 1)

    nchunk = Uc // UB

    def predict(c, i):
        ci = c * nchunk + i
        for j in range(UB):
            u = c * Uc + i * UB + j
            e2c = e2u[0, pl.ds(u, 1), :]
            e2s = e2u[1, pl.ds(u, 1), :]
            a_c = e1u[0]
            a_s = e1u[1]
            tabu[ci, j * T : (j + 1) * T, :] = (a_c * e2c - a_s * e2s).astype(BF16)
            tabu[ci, UBT + j * T : UBT + (j + 1) * T, :] = (-(a_s * e2c + a_c * e2s)).astype(BF16)
        up = jnp.dot(tabu[ci], model_ref[...], preferred_element_type=F32)
        tops, bots = [], []
        for j in range(UB):
            uc = up[j * T : (j + 1) * T]
            us = up[UBT + j * T : UBT + (j + 1) * T]
            tops.append((uc * e1v[0] + us * e1v[1]).astype(BF16))
            bots.append((us * e1v[0] - uc * e1v[1]).astype(BF16))
        both = jnp.concatenate(tops + bots, axis=0)
        b = lax.dot_general(
            both, wv[...], (((1,), (1,)), ((), ())), preferred_element_type=F32
        )
        return b[:UBT] * sgn + swap(b[UBT:])

    def chain(side, d):
        to = lax.rem(me + 1, B) if side == 0 else lax.rem(me + B - 1, B)
        return pltpu.make_async_remote_copy(
            src_ref=sbuf.at[d], dst_ref=s_land.at[side, d],
            send_sem=s_send.at[side, d], recv_sem=s_recv.at[side, d],
            device_id={"bl": to}, device_id_type=pl.DeviceIdType.MESH,
        )

    def passes(side, d):
        return me < d if side == 0 else me > d

    def first(side):
        return me == 0 if side == 0 else me == B - 1

    order = []
    for n in range(B):
        for d in (B - 1 - n, n):
            if d not in order:
                order.append(d)
    for d in order:

        def body(i, carry, d=d):
            rows_i = pl.ds(pl.multiple_of(i * UBT, UBT), UBT)
            sbuf[d, rows_i, :] = predict(d, i).astype(BF16)
            return carry

        lax.fori_loop(0, nchunk, body, 0)
        for side in range(2):
            pl.when(first(side) & passes(side, d))(lambda: chain(side, d).start())

    def pass_on(side, d):
        @pl.when(jnp.logical_not(first(side)) & passes(side, d))
        def _():
            chain(side, d).wait_recv()
            sbuf[d] = (sbuf[d].astype(F32) + s_land[side, d].astype(F32)).astype(BF16)
            chain(side, d).start()

    for n in range(B - 1):
        pass_on(0, B - 1 - n)
        pass_on(1, n)
        if n == 0:
            for copy in scr_copies[1::2]:
                copy.start()

    for copy in obs_copies:
        copy.wait()
    for j in range(nu):
        for b in range(B):
            obsfull[j * T + b * TD : j * T + (b + 1) * TD, :] = obs_land[b, j]
        livefull[j * T : (j + 1) * T, :] = jnp.broadcast_to(
            meta_all[:, 4:5].astype(F32), (T, 2 * G)
        )

    own_copy.wait()
    for copy in scr_copies:
        copy.wait()
    if raw:
        for b in range(B):
            block = jnp.swapaxes(scr_raw[b].astype(F32), 0, 1)
            scr_land[:, b * spd : (b + 1) * spd, :] = block.astype(BF16)
    stations = lax.broadcasted_iota(jnp.int32, (1, B * spd), 1)
    pick = jnp.concatenate([meta_all[:, 2:3], meta_all[:, 3:4]], axis=0) == stations
    pick = jnp.where(pick, 1.0, 0.0).astype(BF16)

    def gains(u, carry):
        both = jnp.dot(pick, scr_land[u], preferred_element_type=F32)
        p = both[:T]
        q = both[T:]
        qsw = swap(q)
        g = p * jnp.where(left, q, qsw) + swap(p) * jnp.where(left, qsw, -q)
        gbuf[pl.ds(pl.multiple_of(u * T, T), T), :] = g
        return carry

    lax.fori_loop(0, Uc, gains, 0)

    sown[...] = sbuf[me].astype(F32)
    for side in range(2):

        @pl.when(jnp.logical_not(first(side)))
        def _(side=side):
            chain(side, me).wait_recv()
            sown[...] += s_land[side, me].astype(F32)

    def contribution(u, carry):
        r = pl.ds(pl.multiple_of(u * T, T), T)
        s = sown[r, :]
        g = gbuf[r, :]
        gsw = swap(g)
        out = s * jnp.where(left, g, gsw) + swap(s) * jnp.where(left, -gsw, g)
        cbuf[r, :] = out.astype(BF16)
        return carry

    lax.fori_loop(0, Uc, contribution, 0)

    def piece(i):
        return pl.ds(pl.multiple_of(i * RPF, RPF), RPF)

    c_copies = [
        pcopy(0, k, cbuf.at[piece(lax.rem(f + k, F))], c_land.at[f]) for k in range(1, F)
    ]
    for copy in c_copies:
        copy.start()
    total = cbuf[piece(f), :].astype(F32)
    for copy in c_copies:
        copy.wait()
    for k in range(1, F):
        total = total + c_land[lax.rem(f + k, F)].astype(F32)
    span = pl.ds(pl.multiple_of((f % per) * RPF, RPF), RPF)
    res = jnp.where(livefull[span, :] > 0.5, obsfull[span, :] - total, 0.0)
    r_land[piece(f), :] = res.astype(BF16)
    res16[...] = res.astype(BF16)
    r_copies = [pcopy(1, k, res16, r_land.at[piece(f)]) for k in range(1, F)]
    for copy in r_copies:
        copy.start()
    if per > 1:
        obsfull[...] = jnp.zeros_like(obsfull)
    obsfull[span, :] = total
    for j in range(nu):
        for b in range(B):
            zsend[b, j] = obsfull[j * T + b * TD : j * T + (b + 1) * TD, :]
    reso[f, me] = zsend[me]
    for copy in r_copies:
        copy.wait()

    def weigh(u, carry):
        r = pl.ds(pl.multiple_of(u * T, T), T)
        x = r_land[r, :].astype(F32)
        g = gbuf[r, :]
        gsw = swap(g)
        out = x * jnp.where(left, g, gsw) + swap(x) * jnp.where(left, gsw, -g)
        rall[me, r, :] = out.astype(BF16)
        return carry

    lax.fori_loop(0, Uc, weigh, 0)

    def right(n):
        block = jnp.maximum(me - n, 0)
        return pltpu.make_async_remote_copy(
            src_ref=rall.at[block], dst_ref=rall.at[block],
            send_sem=w_send.at[0, n], recv_sem=w_recv.at[0, n],
            device_id={"bl": lax.rem(me + 1, B)}, device_id_type=pl.DeviceIdType.MESH,
        )

    def left_(n):
        block = jnp.minimum(me + n, B - 1)
        return pltpu.make_async_remote_copy(
            src_ref=rall.at[block], dst_ref=rall.at[block],
            send_sem=w_send.at[1, n], recv_sem=w_recv.at[1, n],
            device_id={"bl": lax.rem(me + B - 1, B)}, device_id_type=pl.DeviceIdType.MESH,
        )

    def sends_right(n):
        return (me - n >= 0) & (me + 1 < B)

    def sends_left(n):
        return (me + n < B) & (me >= 1)

    pl.when(sends_right(0))(lambda: right(0).start())
    pl.when(sends_left(0))(lambda: left_(0).start())
    z_copies = [
        zcopy(5, k, zsend.at[lax.rem(me + k, B)], reso.at[f, me]) for k in range(1, B)
    ]
    for copy in z_copies:
        copy.start()

    image_ref[...] = jnp.zeros_like(image_ref)

    def image(src):
        def body(i, carry):
            ci = src * nchunk + i
            r = rall[src, pl.ds(pl.multiple_of(i * UBT, UBT), UBT), :].astype(F32)
            both = jnp.concatenate([(r * sgn).astype(BF16), swap(r).astype(BF16)], axis=0)
            prod = jnp.dot(both, wv[...], preferred_element_type=F32)
            tops, bots = [], []
            for j in range(UB):
                pc = prod[j * T : (j + 1) * T]
                ps = prod[UBT + j * T : UBT + (j + 1) * T]
                tops.append((pc * e1v[0] - ps * e1v[1]).astype(BF16))
                bots.append((ps * e1v[0] + pc * e1v[1]).astype(BF16))
            q2 = jnp.concatenate(tops + bots, axis=0)
            image_ref[...] += lax.dot_general(
                tabu[ci], q2, (((0,), (0,)), ((), ())), preferred_element_type=F32
            )
            return carry

        lax.fori_loop(0, nchunk, body, 0)

    image(me)
    for copy in z_copies:
        copy.wait()
    o_copies = [pcopy(2, k, reso.at[f], reso.at[f]) for k in range(1, F)]
    for copy in o_copies:
        copy.start()
    for n in range(B - 1):
        pl.when(me - 1 - n >= 0)(lambda n=n: right(n).wait_recv())
        if n + 1 < B - 1:
            pl.when(sends_right(n + 1))(lambda n=n: right(n + 1).start())
        pl.when(me + 1 + n < B)(lambda n=n: left_(n).wait_recv())
        if n + 1 < B - 1:
            pl.when(sends_left(n + 1))(lambda n=n: left_(n + 1).start())

        def arrived(side, carry, n=n):
            src = jnp.where(side == 0, me - 1 - n, me + 1 + n)
            pl.when((src >= 0) & (src < B))(lambda: image(src))
            return carry

        lax.fori_loop(0, 2, arrived, 0)
    for n in range(B - 1):
        pl.when(sends_right(n))(lambda n=n: right(n).wait_send())
        pl.when(sends_left(n))(lambda n=n: left_(n).wait_send())
    for d in range(B):
        for side in range(2):
            pl.when(passes(side, d))(lambda: chain(side, d).wait_send())
    for copy in o_copies:
        copy.wait()
    group = (me * TD) // RPF if per > 1 else 0
    for g in range(F // per):
        for c in range(B):
            for j in range(nu):
                u = c * Uc + g * nu + j
                pred_ref[pl.ds(u, TD, stride=G), :] = reso[g * per + group, c, j]


def per_device(F, B, facet_model, screens, observed, offsets, stations, counts):
    TD, G = observed.shape[0], observed.shape[1]
    PX = facet_model.shape[2]
    rows = facet_model.shape[1]
    spd = screens.shape[1]
    T = TD * B
    Uc = G // B
    UB = max(1, min(Uc, 384 // T))
    RPF = Uc * T // F
    nu = max(1, RPF // T)
    per = max(1, T // RPF)
    dims = (F, B, T, TD, G, PX, rows, Uc, UB, RPF, nu, per)
    tdp = -(-TD // 8) * 8
    raw = Uc % 16 == 0
    gains = screens[0] if raw else jnp.transpose(screens[0], (1, 0, 2))
    W = 2 * G
    vmem = pl.BlockSpec(memory_space=pltpu.VMEM)
    smem = pl.BlockSpec(memory_space=pltpu.SMEM)
    image, predicted = pl.pallas_call(
        functools.partial(kernel, dims),
        out_shape=(
            jax.ShapeDtypeStruct((rows, PX), F32),
            jax.ShapeDtypeStruct((TD * G, W), F32),
        ),
        in_specs=[smem] * 3 + [vmem] * 3,
        out_specs=(vmem, vmem),
        scratch_shapes=[
            pltpu.VMEM((tdp, 128), jnp.int32),
            pltpu.VMEM((B, tdp, 128), jnp.int32),
            pltpu.VMEM((B, nu, TD, W), F32),
            pltpu.VMEM((T, 128), jnp.int32),
            pltpu.VMEM((2, G, rows), F32),
            pltpu.VMEM((2, T, rows), F32),
            pltpu.VMEM((2, T, PX), F32),
            pltpu.VMEM((W, PX), BF16),
            pltpu.VMEM((G // UB, 2 * UB * T, rows), BF16),
            pltpu.VMEM((B, spd, Uc, W) if raw else (1, 16, 128), BF16),
            pltpu.VMEM((Uc, B * spd, W), BF16),
            pltpu.VMEM((B, Uc * T, W), BF16),
            pltpu.VMEM((2, B, Uc * T, W), BF16),
            pltpu.VMEM((Uc * T, W), F32),
            pltpu.VMEM((Uc * T, W), F32),
            pltpu.VMEM((Uc * T, W), BF16),
            pltpu.VMEM((F, RPF, W), BF16),
            pltpu.VMEM((B, nu, TD, W), F32),
            pltpu.VMEM((nu * T, W), F32),
            pltpu.VMEM((nu * T, W), F32),
            pltpu.VMEM((RPF, W), BF16),
            pltpu.VMEM((Uc * T, W), BF16),
            pltpu.VMEM((B, Uc * T, W), BF16),
            pltpu.VMEM((B, nu, TD, W), F32),
            pltpu.VMEM((F, B, nu, TD, W), F32),
            pltpu.SemaphoreType.DMA((6, B)),
            pltpu.SemaphoreType.DMA((6, B)),
            pltpu.SemaphoreType.DMA((3, F)),
            pltpu.SemaphoreType.DMA((3, F)),
            pltpu.SemaphoreType.DMA((2, B)),
            pltpu.SemaphoreType.DMA((2, B)),
            pltpu.SemaphoreType.DMA((2, B)),
            pltpu.SemaphoreType.DMA((2, B)),
            pltpu.SemaphoreType.DMA,
        ],
        compiler_params=pltpu.CompilerParams(
            collective_id=0, has_side_effects=True, vmem_limit_bytes=56 * 1024 * 1024
        ),
    )(offsets.T, stations.T, counts, facet_model[0], gains, observed.reshape(TD * G, W))
    live = (jnp.arange(TD, dtype=jnp.int32) < counts[0])[:, None, None]
    residual = jnp.where(live, observed - predicted.reshape(TD, G, W), 0.0)
    return (residual, image[None] * (1.0 / (32.0 * G * math.sqrt(T))))


def solution(mesh):
    in_specs = (
        P("facet", "bl", None),
        P("facet", "bl", None, None),
        P("bl", None, None),
        P("bl", None),
        P("bl", None),
        P("bl"),
    )
    out_specs = (P("bl", None, None), P("facet", "bl", None))
    return jax.shard_map(
        functools.partial(per_device, mesh.shape["facet"], mesh.shape["bl"]),
        mesh=mesh, in_specs=in_specs, out_specs=out_specs, check_vma=False,
    )
```

```python
import functools
import math

import jax
import jax.numpy as jnp
from jax import lax
from jax.experimental import pallas as pl
from jax.experimental.pallas import tpu as pltpu
from jax.sharding import PartitionSpec as P

FGRID = 4
F32 = jnp.float32
BF16 = jnp.bfloat16


def cis(k, cells):
    shift = (cells // 4).bit_length() - 1
    turn = (k + cells // 8) >> shift
    x = (k - (turn << shift)).astype(F32) * (2.0 * math.pi / cells)
    y = x * x
    s = x * (1.0 + y * (-1.0 / 6 + y * (1.0 / 120 + y * (-1.0 / 5040 + y * (1.0 / 362880)))))
    c = 1.0 + y * (-0.5 + y * (1.0 / 24 + y * (-1.0 / 720 + y * (1.0 / 40320))))
    odd = (turn & 1) == 1
    cos = jnp.where(odd, s, c)
    sin = jnp.where(odd, c, s)
    cos = jnp.where(((turn + 1) & 2) == 2, -cos, cos)
    sin = jnp.where((turn & 2) == 2, -sin, sin)
    return cos, sin


def kernel(
    dims,
    offsets_ref,
    stations_ref,
    counts_ref,
    model_ref,
    screens_ref,
    obs_ref,
    image_ref,
    pred_ref,
    meta_ref,
    meta_land,
    osend,
    meta_all,
    e2u,
    e1u,
    e1v,
    e2v,
    wv,
    tabv,
    tabu,
    s32,
    scr_raw,
    scr_land,
    sbuf,
    s_land,
    sown,
    gbuf,
    cbuf,
    c_land,
    obs_land,
    obsfull,
    livefull,
    res16,
    r_land,
    rall,
    zsend,
    reso,
    z_send,
    z_recv,
    p_send,
    p_recv,
    w_send,
    w_recv,
    s_send,
    s_recv,
    own_sem,
):
    F, B, T, TD, G, PX, rows, Uc, UB, NT, RPF, nu, per = dims
    N = FGRID * PX
    f = lax.axis_index("facet")
    me = lax.axis_index("bl")
    raw = Uc % 16 == 0
    spd = screens_ref.shape[0 if raw else 1]
    UBT = UB * T
    W = 2 * G
    H = G

    barrier = pltpu.get_barrier_semaphore()
    for k in range(1, B):
        pl.semaphore_signal(
            barrier, inc=1, device_id={"bl": lax.rem(me + k, B)},
            device_id_type=pl.DeviceIdType.MESH,
        )
    for k in range(1, F):
        pl.semaphore_signal(
            barrier, inc=1, device_id={"facet": lax.rem(f + k, F)},
            device_id_type=pl.DeviceIdType.MESH,
        )

    def zcopy(stage, k, src, dst):
        return pltpu.make_async_remote_copy(
            src_ref=src, dst_ref=dst, send_sem=z_send.at[stage, k], recv_sem=z_recv.at[stage, k],
            device_id={"bl": lax.rem(me + k, B)}, device_id_type=pl.DeviceIdType.MESH,
        )

    def pcopy(stage, k, src, dst):
        return pltpu.make_async_remote_copy(
            src_ref=src, dst_ref=dst, send_sem=p_send.at[stage, k], recv_sem=p_recv.at[stage, k],
            device_id={"facet": lax.rem(f + k, F)}, device_id_type=pl.DeviceIdType.MESH,
        )

    def scr_rows(s):
        return pl.ds(pl.multiple_of(s * spd, spd), spd)

    corner_x = (f // FGRID) * PX
    corner_y = (f % FGRID) * PX
    pix_u = lax.broadcasted_iota(jnp.int32, (1, rows), 1) + (corner_x + me * rows)
    pix_v = lax.broadcasted_iota(jnp.int32, (1, PX), 1) + corner_y

    row = lax.broadcasted_iota(jnp.int32, meta_ref.shape, 0)
    col = lax.broadcasted_iota(jnp.int32, meta_ref.shape, 1)
    meta = jnp.where((col == 4) & (row < counts_ref[0]), 1, 0)
    for t in range(TD):
        for j in range(2):
            meta = jnp.where((row == t) & (col == j), offsets_ref[j, t], meta)
            meta = jnp.where((row == t) & (col == j + 2), stations_ref[j, t], meta)
    meta_ref[...] = meta
    for k in range(B):
        c = lax.rem(me + k, B)
        for j in range(nu):
            u = c * Uc + (f // per) * nu + j
            osend[c, j] = obs_ref[pl.ds(u, TD, stride=G), :]

    pl.semaphore_wait(barrier, B + F - 2)

    meta_copies = [zcopy(0, k, meta_ref, meta_land.at[me]) for k in range(1, B)]
    obs_copies = []
    scr_copies = []
    for k in range(1, B):
        c = lax.rem(me + k, B)
        obs_copies.append(zcopy(1, k, osend.at[c], obs_land.at[me]))
        if raw:
            rows_c = pl.ds(pl.multiple_of(c * Uc, Uc), Uc)
            scr_copies.append(zcopy(2, k, screens_ref.at[:, rows_c], scr_raw.at[me]))
        else:
            scr_copies.append(
                zcopy(2, k, screens_ref.at[pl.ds(c * Uc, Uc)], scr_land.at[:, scr_rows(me)])
            )
    for group in (meta_copies, obs_copies, scr_copies[0::2]):
        for copy in group:
            copy.start()
    if raw:
        own_copy = pltpu.make_async_copy(
            screens_ref.at[:, pl.ds(pl.multiple_of(me * Uc, Uc), Uc)], scr_raw.at[me], own_sem
        )
    else:
        own_copy = pltpu.make_async_copy(
            screens_ref.at[pl.ds(me * Uc, Uc)], scr_land.at[:, scr_rows(me)], own_sem
        )
    own_copy.start()
    meta_land[me] = meta_ref[...]
    obs_land[me] = osend[me]

    cells = lax.broadcasted_iota(jnp.int32, (G, 1), 0)
    cu, su = cis(cells * pix_u, N)
    e2u[0] = cu
    e2u[1] = su
    for j in range(0, PX, 256):
        cv, sv = cis(cells * pix_v[:, j : j + 256], N)
        e2v[0, :, j : j + 256] = cv
        e2v[1, :, j : j + 256] = sv
        wv[:H, j : j + 256] = cv.astype(BF16)
        wv[H:, j : j + 256] = sv.astype(BF16)

    for copy in meta_copies:
        copy.wait()
    for b in range(B):
        meta_all[b * TD : (b + 1) * TD, :] = meta_land[b, :TD, :]
    ou = meta_all[:, 0:1]
    ov = meta_all[:, 1:2]
    c1, s1 = cis(ou * pix_u, N)
    e1u[0] = c1
    e1u[1] = s1
    for j in range(0, PX, 256):
        c1, s1 = cis(ov * pix_v[:, j : j + 256], N)
        e1v[0, :, j : j + 256] = c1
        e1v[1, :, j : j + 256] = s1

    lane = lax.broadcasted_iota(jnp.int32, (1, 2 * G), 1)
    left = lane < G
    sgn = jnp.where(left, 1.0, -1.0).astype(F32)

    def swap(x):
        return pltpu.roll(x, G, 1)

    nchunk = Uc // UB

    def predict(g, carry):
        for j in range(NT):
            t = g * NT + j
            a_c = e1v[0, pl.ds(t, 1), :]
            a_s = e1v[1, pl.ds(t, 1), :]
            tabv[j * W : j * W + H, :] = (a_c * e2v[0] - a_s * e2v[1]).astype(BF16)
            tabv[j * W + H : (j + 1) * W, :] = (a_s * e2v[0] + a_c * e2v[1]).astype(BF16)
        x = lax.dot_general(
            tabv[...], model_ref[...], (((1,), (1,)), ((), ())), preferred_element_type=F32
        ).astype(BF16)
        for j in range(NT):
            t = g * NT + j
            a_c = e1u[0, pl.ds(t, 1), :]
            a_s = e1u[1, pl.ds(t, 1), :]
            top = (a_c * e2u[0] - a_s * e2u[1]).astype(BF16)
            bot = (-(a_s * e2u[0] + a_c * e2u[1])).astype(BF16)
            b = lax.dot_general(
                jnp.concatenate([top, bot], axis=0), x[j * W : (j + 1) * W],
                (((1,), (1,)), ((), ())), preferred_element_type=F32,
            )
            s32[pl.ds(t, G, stride=T), :] = b[:H] * sgn + swap(b[H:])
        return carry

    lax.fori_loop(0, T // NT, predict, 0)

    def image_table(ci, carry):
        for j in range(UB):
            u = ci * UB + j
            e2c = e2u[0, pl.ds(u, 1), :]
            e2s = e2u[1, pl.ds(u, 1), :]
            a_c = e1u[0]
            a_s = e1u[1]
            tabu[ci, j * T : (j + 1) * T, :] = (a_c * e2c - a_s * e2s).astype(BF16)
            tabu[ci, UBT + j * T : UBT + (j + 1) * T, :] = (-(a_s * e2c + a_c * e2s)).astype(BF16)
        return carry

    def chain(side, d):
        to = lax.rem(me + 1, B) if side == 0 else lax.rem(me + B - 1, B)
        return pltpu.make_async_remote_copy(
            src_ref=sbuf.at[d], dst_ref=s_land.at[side, d],
            send_sem=s_send.at[side, d], recv_sem=s_recv.at[side, d],
            device_id={"bl": to}, device_id_type=pl.DeviceIdType.MESH,
        )

    def passes(side, d):
        return me < d if side == 0 else me > d

    def first(side):
        return me == 0 if side == 0 else me == B - 1

    order = []
    for n in range(B):
        for d in (B - 1 - n, n):
            if d not in order:
                order.append(d)
    for d in order:
        sbuf[d] = s32[d * Uc * T : (d + 1) * Uc * T, :].astype(BF16)
        for side in range(2):
            pl.when(first(side) & passes(side, d))(lambda: chain(side, d).start())

    def pass_on(side, d):
        @pl.when(jnp.logical_not(first(side)) & passes(side, d))
        def _():
            chain(side, d).wait_recv()
            sbuf[d] = (sbuf[d].astype(F32) + s_land[side, d].astype(F32)).astype(BF16)
            chain(side, d).start()

    for n in range(B - 1):
        pass_on(0, B - 1 - n)
        pass_on(1, n)
        if n == 0:
            for copy in scr_copies[1::2]:
                copy.start()

    for copy in obs_copies:
        copy.wait()
    for j in range(nu):
        for b in range(B):
            obsfull[j * T + b * TD : j * T + (b + 1) * TD, :] = obs_land[b, j]
        livefull[j * T : (j + 1) * T, :] = jnp.broadcast_to(
            meta_all[:, 4:5].astype(F32), (T, 2 * G)
        )

    own_copy.wait()
    for copy in scr_copies:
        copy.wait()
    if raw:
        for b in range(B):
            block = jnp.swapaxes(scr_raw[b].astype(F32), 0, 1)
            scr_land[:, b * spd : (b + 1) * spd, :] = block.astype(BF16)
    stations = lax.broadcasted_iota(jnp.int32, (1, B * spd), 1)
    pick = jnp.concatenate([meta_all[:, 2:3], meta_all[:, 3:4]], axis=0) == stations
    pick = jnp.where(pick, 1.0, 0.0).astype(BF16)

    def gains(u, carry):
        both = jnp.dot(pick, scr_land[u], preferred_element_type=F32)
        p = both[:T]
        q = both[T:]
        qsw = swap(q)
        g = p * jnp.where(left, q, qsw) + swap(p) * jnp.where(left, qsw, -q)
        gbuf[pl.ds(pl.multiple_of(u * T, T), T), :] = g
        return carry

    lax.fori_loop(0, Uc, gains, 0)

    sown[...] = sbuf[me].astype(F32)
    for side in range(2):

        @pl.when(jnp.logical_not(first(side)))
        def _(side=side):
            chain(side, me).wait_recv()
            sown[...] += s_land[side, me].astype(F32)

    def contribution(u, carry):
        r = pl.ds(pl.multiple_of(u * T, T), T)
        s = sown[r, :]
        g = gbuf[r, :]
        gsw = swap(g)
        out = s * jnp.where(left, g, gsw) + swap(s) * jnp.where(left, -gsw, g)
        cbuf[r, :] = out.astype(BF16)
        return carry

    lax.fori_loop(0, Uc, contribution, 0)

    def piece(i):
        return pl.ds(pl.multiple_of(i * RPF, RPF), RPF)

    c_copies = [
        pcopy(0, k, cbuf.at[piece(lax.rem(f + k, F))], c_land.at[f]) for k in range(1, F)
    ]
    for copy in c_copies:
        copy.start()
    lax.fori_loop(0, G // UB, image_table, 0)
    total = cbuf[piece(f), :].astype(F32)
    for copy in c_copies:
        copy.wait()
    for k in range(1, F):
        total = total + c_land[lax.rem(f + k, F)].astype(F32)
    span = pl.ds(pl.multiple_of((f % per) * RPF, RPF), RPF)
    res = jnp.where(livefull[span, :] > 0.5, obsfull[span, :] - total, 0.0)
    r_land[piece(f), :] = res.astype(BF16)
    res16[...] = res.astype(BF16)
    r_copies = [pcopy(1, k, res16, r_land.at[piece(f)]) for k in range(1, F)]
    for copy in r_copies:
        copy.start()
    if per > 1:
        obsfull[...] = jnp.zeros_like(obsfull)
    obsfull[span, :] = total
    for j in range(nu):
        for b in range(B):
            zsend[b, j] = obsfull[j * T + b * TD : j * T + (b + 1) * TD, :]
    reso[f, me] = zsend[me]
    for copy in r_copies:
        copy.wait()

    def weigh(u, carry):
        r = pl.ds(pl.multiple_of(u * T, T), T)
        x = r_land[r, :].astype(F32)
        g = gbuf[r, :]
        gsw = swap(g)
        out = x * jnp.where(left, g, gsw) + swap(x) * jnp.where(left, gsw, -g)
        rall[me, r, :] = out.astype(BF16)
        return carry

    lax.fori_loop(0, Uc, weigh, 0)

    def right(n):
        block = jnp.maximum(me - n, 0)
        return pltpu.make_async_remote_copy(
            src_ref=rall.at[block], dst_ref=rall.at[block],
            send_sem=w_send.at[0, n], recv_sem=w_recv.at[0, n],
            device_id={"bl": lax.rem(me + 1, B)}, device_id_type=pl.DeviceIdType.MESH,
        )

    def left_(n):
        block = jnp.minimum(me + n, B - 1)
        return pltpu.make_async_remote_copy(
            src_ref=rall.at[block], dst_ref=rall.at[block],
            send_sem=w_send.at[1, n], recv_sem=w_recv.at[1, n],
            device_id={"bl": lax.rem(me + B - 1, B)}, device_id_type=pl.DeviceIdType.MESH,
        )

    def sends_right(n):
        return (me - n >= 0) & (me + 1 < B)

    def sends_left(n):
        return (me + n < B) & (me >= 1)

    pl.when(sends_right(0))(lambda: right(0).start())
    pl.when(sends_left(0))(lambda: left_(0).start())
    z_copies = [
        zcopy(5, k, zsend.at[lax.rem(me + k, B)], reso.at[f, me]) for k in range(1, B)
    ]
    for copy in z_copies:
        copy.start()

    image_ref[...] = jnp.zeros_like(image_ref)

    def image(src):
        def body(i, carry):
            ci = src * nchunk + i
            r = rall[src, pl.ds(pl.multiple_of(i * UBT, UBT), UBT), :].astype(F32)
            both = jnp.concatenate([(r * sgn).astype(BF16), swap(r).astype(BF16)], axis=0)
            prod = jnp.dot(both, wv[...], preferred_element_type=F32)
            tops, bots = [], []
            for j in range(UB):
                pc = prod[j * T : (j + 1) * T]
                ps = prod[UBT + j * T : UBT + (j + 1) * T]
                tops.append((pc * e1v[0] - ps * e1v[1]).astype(BF16))
                bots.append((ps * e1v[0] + pc * e1v[1]).astype(BF16))
            q2 = jnp.concatenate(tops + bots, axis=0)
            image_ref[...] += lax.dot_general(
                tabu[ci], q2, (((0,), (0,)), ((), ())), preferred_element_type=F32
            )
            return carry

        lax.fori_loop(0, nchunk, body, 0)

    image(me)
    for copy in z_copies:
        copy.wait()
    o_copies = [pcopy(2, k, reso.at[f], reso.at[f]) for k in range(1, F)]
    for copy in o_copies:
        copy.start()
    for n in range(B - 1):
        pl.when(me - 1 - n >= 0)(lambda n=n: right(n).wait_recv())
        if n + 1 < B - 1:
            pl.when(sends_right(n + 1))(lambda n=n: right(n + 1).start())
        pl.when(me + 1 + n < B)(lambda n=n: left_(n).wait_recv())
        if n + 1 < B - 1:
            pl.when(sends_left(n + 1))(lambda n=n: left_(n + 1).start())

        def arrived(side, carry, n=n):
            src = jnp.where(side == 0, me - 1 - n, me + 1 + n)
            pl.when((src >= 0) & (src < B))(lambda: image(src))
            return carry

        lax.fori_loop(0, 2, arrived, 0)
    for n in range(B - 1):
        pl.when(sends_right(n))(lambda n=n: right(n).wait_send())
        pl.when(sends_left(n))(lambda n=n: left_(n).wait_send())
    for d in range(B):
        for side in range(2):
            pl.when(passes(side, d))(lambda: chain(side, d).wait_send())
    for copy in o_copies:
        copy.wait()
    group = (me * TD) // RPF if per > 1 else 0
    for g in range(F // per):
        for c in range(B):
            for j in range(nu):
                u = c * Uc + g * nu + j
                pred_ref[pl.ds(u, TD, stride=G), :] = reso[g * per + group, c, j]


def per_device(F, B, facet_model, screens, observed, offsets, stations, counts):
    TD, G = observed.shape[0], observed.shape[1]
    PX = facet_model.shape[2]
    rows = facet_model.shape[1]
    spd = screens.shape[1]
    T = TD * B
    Uc = G // B
    UB = max(1, min(Uc, 384 // T))
    NT = 4 if T % 4 == 0 else 1
    RPF = Uc * T // F
    nu = max(1, RPF // T)
    per = max(1, T // RPF)
    dims = (F, B, T, TD, G, PX, rows, Uc, UB, NT, RPF, nu, per)
    tdp = -(-TD // 8) * 8
    raw = Uc % 16 == 0
    gains = screens[0] if raw else jnp.transpose(screens[0], (1, 0, 2))
    W = 2 * G
    vmem = pl.BlockSpec(memory_space=pltpu.VMEM)
    smem = pl.BlockSpec(memory_space=pltpu.SMEM)
    image, predicted = pl.pallas_call(
        functools.partial(kernel, dims),
        out_shape=(
            jax.ShapeDtypeStruct((rows, PX), F32),
            jax.ShapeDtypeStruct((TD * G, W), F32),
        ),
        in_specs=[smem] * 3 + [vmem] * 3,
        out_specs=(vmem, vmem),
        scratch_shapes=[
            pltpu.VMEM((tdp, 128), jnp.int32),
            pltpu.VMEM((B, tdp, 128), jnp.int32),
            pltpu.VMEM((B, nu, TD, W), F32),
            pltpu.VMEM((T, 128), jnp.int32),
            pltpu.VMEM((2, G, rows), F32),
            pltpu.VMEM((2, T, rows), F32),
            pltpu.VMEM((2, T, PX), F32),
            pltpu.VMEM((2, G, PX), F32),
            pltpu.VMEM((W, PX), BF16),
            pltpu.VMEM((NT * W, PX), BF16),
            pltpu.VMEM((G // UB, 2 * UB * T, rows), BF16),
            pltpu.VMEM((G * T, W), F32),
            pltpu.VMEM((B, spd, Uc, W) if raw else (1, 16, 128), BF16),
            pltpu.VMEM((Uc, B * spd, W), BF16),
            pltpu.VMEM((B, Uc * T, W), BF16),
            pltpu.VMEM((2, B, Uc * T, W), BF16),
            pltpu.VMEM((Uc * T, W), F32),
            pltpu.VMEM((Uc * T, W), F32),
            pltpu.VMEM((Uc * T, W), BF16),
            pltpu.VMEM((F, RPF, W), BF16),
            pltpu.VMEM((B, nu, TD, W), F32),
            pltpu.VMEM((nu * T, W), F32),
            pltpu.VMEM((nu * T, W), F32),
            pltpu.VMEM((RPF, W), BF16),
            pltpu.VMEM((Uc * T, W), BF16),
            pltpu.VMEM((B, Uc * T, W), BF16),
            pltpu.VMEM((B, nu, TD, W), F32),
            pltpu.VMEM((F, B, nu, TD, W), F32),
            pltpu.SemaphoreType.DMA((6, B)),
            pltpu.SemaphoreType.DMA((6, B)),
            pltpu.SemaphoreType.DMA((3, F)),
            pltpu.SemaphoreType.DMA((3, F)),
            pltpu.SemaphoreType.DMA((2, B)),
            pltpu.SemaphoreType.DMA((2, B)),
            pltpu.SemaphoreType.DMA((2, B)),
            pltpu.SemaphoreType.DMA((2, B)),
            pltpu.SemaphoreType.DMA,
        ],
        compiler_params=pltpu.CompilerParams(
            collective_id=0, has_side_effects=True, vmem_limit_bytes=56 * 1024 * 1024
        ),
    )(offsets.T, stations.T, counts, facet_model[0], gains, observed.reshape(TD * G, W))
    live = (jnp.arange(TD, dtype=jnp.int32) < counts[0])[:, None, None]
    residual = jnp.where(live, observed - predicted.reshape(TD, G, W), 0.0)
    return (residual, image[None] * (1.0 / (32.0 * G * math.sqrt(T))))


def solution(mesh):
    in_specs = (
        P("facet", "bl", None),
        P("facet", "bl", None, None),
        P("bl", None, None),
        P("bl", None),
        P("bl", None),
        P("bl"),
    )
    out_specs = (P("bl", None, None), P("facet", "bl", None))
    return jax.shard_map(
        functools.partial(per_device, mesh.shape["facet"], mesh.shape["bl"]),
        mesh=mesh, in_specs=in_specs, out_specs=out_specs, check_vma=False,
    )
```

```python
import functools
import math

import jax
import jax.numpy as jnp
from jax import lax
from jax.experimental import pallas as pl
from jax.experimental.pallas import tpu as pltpu
from jax.sharding import PartitionSpec as P

FGRID = 4
F32 = jnp.float32
BF16 = jnp.bfloat16


def cis(k, cells):
    shift = (cells // 4).bit_length() - 1
    turn = (k + cells // 8) >> shift
    x = (k - (turn << shift)).astype(F32) * (2.0 * math.pi / cells)
    y = x * x
    s = x * (1.0 + y * (-1.0 / 6 + y * (1.0 / 120 + y * (-1.0 / 5040 + y * (1.0 / 362880)))))
    c = 1.0 + y * (-0.5 + y * (1.0 / 24 + y * (-1.0 / 720 + y * (1.0 / 40320))))
    odd = (turn & 1) == 1
    cos = jnp.where(odd, s, c)
    sin = jnp.where(odd, c, s)
    cos = jnp.where(((turn + 1) & 2) == 2, -cos, cos)
    sin = jnp.where((turn & 2) == 2, -sin, sin)
    return cos, sin


def kernel(
    dims,
    offsets_ref,
    stations_ref,
    counts_ref,
    model_ref,
    screens_ref,
    obs_ref,
    image_ref,
    pred_ref,
    meta_ref,
    meta_land,
    osend,
    meta_all,
    e2u,
    e1u,
    e1v,
    e2v,
    wv,
    tabv,
    tabu,
    s32,
    scr_raw,
    scr_land,
    sbuf,
    s_land,
    sown,
    gbuf,
    cbuf,
    c_land,
    obs_land,
    obsfull,
    livefull,
    res16,
    r_land,
    rall,
    zsend,
    reso,
    z_send,
    z_recv,
    p_send,
    p_recv,
    w_send,
    w_recv,
    s_send,
    s_recv,
    own_sem,
):
    F, B, T, TD, G, PX, rows, Uc, UB, NT, RPF, nu, per = dims
    N = FGRID * PX
    f = lax.axis_index("facet")
    me = lax.axis_index("bl")
    raw = Uc % 16 == 0
    spd = screens_ref.shape[0 if raw else 1]
    UBT = UB * T
    W = 2 * G
    H = G

    barrier = pltpu.get_barrier_semaphore()
    for k in range(1, B):
        pl.semaphore_signal(
            barrier, inc=1, device_id={"bl": lax.rem(me + k, B)},
            device_id_type=pl.DeviceIdType.MESH,
        )
    for k in range(1, F):
        pl.semaphore_signal(
            barrier, inc=1, device_id={"facet": lax.rem(f + k, F)},
            device_id_type=pl.DeviceIdType.MESH,
        )

    def zcopy(stage, k, src, dst):
        return pltpu.make_async_remote_copy(
            src_ref=src, dst_ref=dst, send_sem=z_send.at[stage, k], recv_sem=z_recv.at[stage, k],
            device_id={"bl": lax.rem(me + k, B)}, device_id_type=pl.DeviceIdType.MESH,
        )

    def pcopy(stage, k, src, dst):
        return pltpu.make_async_remote_copy(
            src_ref=src, dst_ref=dst, send_sem=p_send.at[stage, k], recv_sem=p_recv.at[stage, k],
            device_id={"facet": lax.rem(f + k, F)}, device_id_type=pl.DeviceIdType.MESH,
        )

    def scr_rows(s):
        return pl.ds(pl.multiple_of(s * spd, spd), spd)

    corner_x = (f // FGRID) * PX
    corner_y = (f % FGRID) * PX
    pix_u = lax.broadcasted_iota(jnp.int32, (1, rows), 1) + (corner_x + me * rows)
    pix_v = lax.broadcasted_iota(jnp.int32, (1, PX), 1) + corner_y

    row = lax.broadcasted_iota(jnp.int32, meta_ref.shape, 0)
    col = lax.broadcasted_iota(jnp.int32, meta_ref.shape, 1)
    meta = jnp.where((col == 4) & (row < counts_ref[0]), 1, 0)
    for t in range(TD):
        for j in range(2):
            meta = jnp.where((row == t) & (col == j), offsets_ref[j, t], meta)
            meta = jnp.where((row == t) & (col == j + 2), stations_ref[j, t], meta)
    meta_ref[...] = meta
    for k in range(B):
        c = lax.rem(me + k, B)
        for j in range(nu):
            u = c * Uc + (f // per) * nu + j
            osend[c, j] = obs_ref[pl.ds(u, TD, stride=G), :]

    pl.semaphore_wait(barrier, B + F - 2)

    meta_copies = [zcopy(0, k, meta_ref, meta_land.at[me]) for k in range(1, B)]
    obs_copies = []
    scr_copies = []
    for k in range(1, B):
        c = lax.rem(me + k, B)
        obs_copies.append(zcopy(1, k, osend.at[c], obs_land.at[me]))
        if raw:
            rows_c = pl.ds(pl.multiple_of(c * Uc, Uc), Uc)
            scr_copies.append(zcopy(2, k, screens_ref.at[:, rows_c], scr_raw.at[me]))
        else:
            scr_copies.append(
                zcopy(2, k, screens_ref.at[pl.ds(c * Uc, Uc)], scr_land.at[:, scr_rows(me)])
            )
    for group in (meta_copies, obs_copies, scr_copies[0::2]):
        for copy in group:
            copy.start()
    if raw:
        own_copy = pltpu.make_async_copy(
            screens_ref.at[:, pl.ds(pl.multiple_of(me * Uc, Uc), Uc)], scr_raw.at[me], own_sem
        )
    else:
        own_copy = pltpu.make_async_copy(
            screens_ref.at[pl.ds(me * Uc, Uc)], scr_land.at[:, scr_rows(me)], own_sem
        )
    own_copy.start()
    meta_land[me] = meta_ref[...]
    obs_land[me] = osend[me]

    cells = lax.broadcasted_iota(jnp.int32, (G, 1), 0)
    cu, su = cis(cells * pix_u, N)
    e2u[0] = cu
    e2u[1] = su
    for j in range(0, PX, 256):
        cv, sv = cis(cells * pix_v[:, j : j + 256], N)
        e2v[0, :, j : j + 256] = cv
        e2v[1, :, j : j + 256] = sv
        wv[:H, j : j + 256] = cv.astype(BF16)
        wv[H:, j : j + 256] = sv.astype(BF16)

    for copy in meta_copies:
        copy.wait()
    for b in range(B):
        meta_all[b * TD : (b + 1) * TD, :] = meta_land[b, :TD, :]
    ou = meta_all[:, 0:1]
    ov = meta_all[:, 1:2]
    c1, s1 = cis(ou * pix_u, N)
    e1u[0] = c1
    e1u[1] = s1
    for j in range(0, PX, 256):
        c1, s1 = cis(ov * pix_v[:, j : j + 256], N)
        e1v[0, :, j : j + 256] = c1
        e1v[1, :, j : j + 256] = s1

    lane = lax.broadcasted_iota(jnp.int32, (1, 2 * G), 1)
    left = lane < G
    sgn = jnp.where(left, 1.0, -1.0).astype(F32)

    def swap(x):
        return pltpu.roll(x, G, 1)

    nchunk = Uc // UB

    def predict(g, carry):
        for j in range(NT):
            t = g * NT + j
            a_c = e1v[0, pl.ds(t, 1), :]
            a_s = e1v[1, pl.ds(t, 1), :]
            tabv[j * W : j * W + H, :] = (a_c * e2v[0] - a_s * e2v[1]).astype(BF16)
            tabv[j * W + H : (j + 1) * W, :] = (a_s * e2v[0] + a_c * e2v[1]).astype(BF16)
        x = lax.dot_general(
            tabv[...], model_ref[...], (((1,), (1,)), ((), ())), preferred_element_type=F32
        ).astype(BF16)
        for j in range(NT):
            t = g * NT + j
            a_c = e1u[0, pl.ds(t, 1), :]
            a_s = e1u[1, pl.ds(t, 1), :]
            top = (a_c * e2u[0] - a_s * e2u[1]).astype(BF16)
            bot = (-(a_s * e2u[0] + a_c * e2u[1])).astype(BF16)
            b = lax.dot_general(
                jnp.concatenate([top, bot], axis=0), x[j * W : (j + 1) * W],
                (((1,), (1,)), ((), ())), preferred_element_type=F32,
            )
            s32[pl.ds(t, G, stride=T), :] = b[:H] * sgn + swap(b[H:])
        return carry

    lax.fori_loop(0, T // NT, predict, 0)

    def image_table(ci, carry):
        for j in range(UB):
            u = ci * UB + j
            e2c = e2u[0, pl.ds(u, 1), :]
            e2s = e2u[1, pl.ds(u, 1), :]
            a_c = e1u[0]
            a_s = e1u[1]
            tabu[ci, j * T : (j + 1) * T, :] = (a_c * e2c - a_s * e2s).astype(BF16)
            tabu[ci, UBT + j * T : UBT + (j + 1) * T, :] = (-(a_s * e2c + a_c * e2s)).astype(BF16)
        return carry

    def chain(side, d):
        to = lax.rem(me + 1, B) if side == 0 else lax.rem(me + B - 1, B)
        return pltpu.make_async_remote_copy(
            src_ref=sbuf.at[d], dst_ref=s_land.at[side, d],
            send_sem=s_send.at[side, d], recv_sem=s_recv.at[side, d],
            device_id={"bl": to}, device_id_type=pl.DeviceIdType.MESH,
        )

    def passes(side, d):
        return me < d if side == 0 else me > d

    def first(side):
        return me == 0 if side == 0 else me == B - 1

    order = []
    for n in range(B):
        for d in (B - 1 - n, n):
            if d not in order:
                order.append(d)
    for d in order:
        sbuf[d] = s32[d * Uc * T : (d + 1) * Uc * T, :].astype(BF16)
        for side in range(2):
            pl.when(first(side) & passes(side, d))(lambda: chain(side, d).start())

    def pass_on(side, d):
        @pl.when(jnp.logical_not(first(side)) & passes(side, d))
        def _():
            chain(side, d).wait_recv()
            sbuf[d] = (sbuf[d].astype(F32) + s_land[side, d].astype(F32)).astype(BF16)
            chain(side, d).start()

    for copy in scr_copies[1::2]:
        copy.start()

    def stand(b):
        if raw:
            block = jnp.swapaxes(scr_raw[b].astype(F32), 0, 1)
            scr_land[:, scr_rows(b), :] = block.astype(BF16)

    own_copy.wait()
    stand(me)
    early = list(range(1, B, 2))
    for n in range(B - 1):
        pass_on(0, B - 1 - n)
        pass_on(1, n)
        if early:
            k = early.pop(0)
            scr_copies[k - 1].wait()
            stand(lax.rem(me + B - k, B))

    for copy in obs_copies:
        copy.wait()
    for j in range(nu):
        for b in range(B):
            obsfull[j * T + b * TD : j * T + (b + 1) * TD, :] = obs_land[b, j]
        livefull[j * T : (j + 1) * T, :] = jnp.broadcast_to(
            meta_all[:, 4:5].astype(F32), (T, 2 * G)
        )

    for k in range(2, B, 2):
        scr_copies[k - 1].wait()
        stand(lax.rem(me + B - k, B))
    stations = lax.broadcasted_iota(jnp.int32, (1, B * spd), 1)
    pick = jnp.concatenate([meta_all[:, 2:3], meta_all[:, 3:4]], axis=0) == stations
    pick = jnp.where(pick, 1.0, 0.0).astype(BF16)

    def gains(u, carry):
        both = jnp.dot(pick, scr_land[u], preferred_element_type=F32)
        p = both[:T]
        q = both[T:]
        qsw = swap(q)
        g = p * jnp.where(left, q, qsw) + swap(p) * jnp.where(left, qsw, -q)
        gbuf[pl.ds(pl.multiple_of(u * T, T), T), :] = g
        return carry

    lax.fori_loop(0, Uc, gains, 0, unroll=4)

    sown[...] = sbuf[me].astype(F32)
    for side in range(2):

        @pl.when(jnp.logical_not(first(side)))
        def _(side=side):
            chain(side, me).wait_recv()
            sown[...] += s_land[side, me].astype(F32)

    def contribution(u, carry):
        r = pl.ds(pl.multiple_of(u * T, T), T)
        s = sown[r, :]
        g = gbuf[r, :]
        gsw = swap(g)
        out = s * jnp.where(left, g, gsw) + swap(s) * jnp.where(left, -gsw, g)
        cbuf[r, :] = out.astype(BF16)
        return carry

    lax.fori_loop(0, Uc, contribution, 0, unroll=4)

    def piece(i):
        return pl.ds(pl.multiple_of(i * RPF, RPF), RPF)

    c_copies = [
        pcopy(0, k, cbuf.at[piece(lax.rem(f + k, F))], c_land.at[f]) for k in range(1, F)
    ]
    for copy in c_copies:
        copy.start()
    lax.fori_loop(0, G // UB, image_table, 0)
    total = cbuf[piece(f), :].astype(F32)
    for copy in c_copies:
        copy.wait()
    for k in range(1, F):
        total = total + c_land[lax.rem(f + k, F)].astype(F32)
    span = pl.ds(pl.multiple_of((f % per) * RPF, RPF), RPF)
    res = jnp.where(livefull[span, :] > 0.5, obsfull[span, :] - total, 0.0)
    r_land[piece(f), :] = res.astype(BF16)
    res16[...] = res.astype(BF16)
    r_copies = [pcopy(1, k, res16, r_land.at[piece(f)]) for k in range(1, F)]
    for copy in r_copies:
        copy.start()
    if per > 1:
        obsfull[...] = jnp.zeros_like(obsfull)
    obsfull[span, :] = total
    for j in range(nu):
        for b in range(B):
            zsend[b, j] = obsfull[j * T + b * TD : j * T + (b + 1) * TD, :]
    reso[f, me] = zsend[me]
    for copy in r_copies:
        copy.wait()

    def weigh(u, carry):
        r = pl.ds(pl.multiple_of(u * T, T), T)
        x = r_land[r, :].astype(F32)
        g = gbuf[r, :]
        gsw = swap(g)
        out = x * jnp.where(left, g, gsw) + swap(x) * jnp.where(left, gsw, -g)
        rall[me, r, :] = out.astype(BF16)
        return carry

    lax.fori_loop(0, Uc, weigh, 0, unroll=4)

    def right(n):
        block = jnp.maximum(me - n, 0)
        return pltpu.make_async_remote_copy(
            src_ref=rall.at[block], dst_ref=rall.at[block],
            send_sem=w_send.at[0, n], recv_sem=w_recv.at[0, n],
            device_id={"bl": lax.rem(me + 1, B)}, device_id_type=pl.DeviceIdType.MESH,
        )

    def left_(n):
        block = jnp.minimum(me + n, B - 1)
        return pltpu.make_async_remote_copy(
            src_ref=rall.at[block], dst_ref=rall.at[block],
            send_sem=w_send.at[1, n], recv_sem=w_recv.at[1, n],
            device_id={"bl": lax.rem(me + B - 1, B)}, device_id_type=pl.DeviceIdType.MESH,
        )

    def sends_right(n):
        return (me - n >= 0) & (me + 1 < B)

    def sends_left(n):
        return (me + n < B) & (me >= 1)

    pl.when(sends_right(0))(lambda: right(0).start())
    pl.when(sends_left(0))(lambda: left_(0).start())
    z_copies = [
        zcopy(5, k, zsend.at[lax.rem(me + k, B)], reso.at[f, me]) for k in range(1, B)
    ]
    for copy in z_copies:
        copy.start()

    image_ref[...] = jnp.zeros_like(image_ref)

    def image(src):
        def body(i, carry):
            ci = src * nchunk + i
            r = rall[src, pl.ds(pl.multiple_of(i * UBT, UBT), UBT), :].astype(F32)
            both = jnp.concatenate([(r * sgn).astype(BF16), swap(r).astype(BF16)], axis=0)
            prod = jnp.dot(both, wv[...], preferred_element_type=F32)
            tops, bots = [], []
            for j in range(UB):
                pc = prod[j * T : (j + 1) * T]
                ps = prod[UBT + j * T : UBT + (j + 1) * T]
                tops.append((pc * e1v[0] - ps * e1v[1]).astype(BF16))
                bots.append((ps * e1v[0] + pc * e1v[1]).astype(BF16))
            q2 = jnp.concatenate(tops + bots, axis=0)
            image_ref[...] += lax.dot_general(
                tabu[ci], q2, (((0,), (0,)), ((), ())), preferred_element_type=F32
            )
            return carry

        lax.fori_loop(0, nchunk, body, 0)

    image(me)
    for copy in z_copies:
        copy.wait()
    o_copies = [pcopy(2, k, reso.at[f], reso.at[f]) for k in range(1, F)]
    for copy in o_copies:
        copy.start()
    for n in range(B - 1):
        pl.when(me - 1 - n >= 0)(lambda n=n: right(n).wait_recv())
        if n + 1 < B - 1:
            pl.when(sends_right(n + 1))(lambda n=n: right(n + 1).start())
        pl.when(me + 1 + n < B)(lambda n=n: left_(n).wait_recv())
        if n + 1 < B - 1:
            pl.when(sends_left(n + 1))(lambda n=n: left_(n + 1).start())

        def arrived(side, carry, n=n):
            src = jnp.where(side == 0, me - 1 - n, me + 1 + n)
            pl.when((src >= 0) & (src < B))(lambda: image(src))
            return carry

        lax.fori_loop(0, 2, arrived, 0)
    for n in range(B - 1):
        pl.when(sends_right(n))(lambda n=n: right(n).wait_send())
        pl.when(sends_left(n))(lambda n=n: left_(n).wait_send())
    for d in range(B):
        for side in range(2):
            pl.when(passes(side, d))(lambda: chain(side, d).wait_send())
    for copy in o_copies:
        copy.wait()
    group = (me * TD) // RPF if per > 1 else 0
    for g in range(F // per):
        for c in range(B):
            for j in range(nu):
                u = c * Uc + g * nu + j
                pred_ref[pl.ds(u, TD, stride=G), :] = reso[g * per + group, c, j]


def per_device(F, B, facet_model, screens, observed, offsets, stations, counts):
    TD, G = observed.shape[0], observed.shape[1]
    PX = facet_model.shape[2]
    rows = facet_model.shape[1]
    spd = screens.shape[1]
    T = TD * B
    Uc = G // B
    UB = max(1, min(Uc, 384 // T))
    NT = 4 if T % 4 == 0 else 1
    RPF = Uc * T // F
    nu = max(1, RPF // T)
    per = max(1, T // RPF)
    dims = (F, B, T, TD, G, PX, rows, Uc, UB, NT, RPF, nu, per)
    tdp = -(-TD // 8) * 8
    raw = Uc % 16 == 0
    gains = screens[0] if raw else jnp.transpose(screens[0], (1, 0, 2))
    W = 2 * G
    vmem = pl.BlockSpec(memory_space=pltpu.VMEM)
    smem = pl.BlockSpec(memory_space=pltpu.SMEM)
    image, predicted = pl.pallas_call(
        functools.partial(kernel, dims),
        out_shape=(
            jax.ShapeDtypeStruct((rows, PX), F32),
            jax.ShapeDtypeStruct((TD * G, W), F32),
        ),
        in_specs=[smem] * 3 + [vmem] * 3,
        out_specs=(vmem, vmem),
        scratch_shapes=[
            pltpu.VMEM((tdp, 128), jnp.int32),
            pltpu.VMEM((B, tdp, 128), jnp.int32),
            pltpu.VMEM((B, nu, TD, W), F32),
            pltpu.VMEM((T, 128), jnp.int32),
            pltpu.VMEM((2, G, rows), F32),
            pltpu.VMEM((2, T, rows), F32),
            pltpu.VMEM((2, T, PX), F32),
            pltpu.VMEM((2, G, PX), F32),
            pltpu.VMEM((W, PX), BF16),
            pltpu.VMEM((NT * W, PX), BF16),
            pltpu.VMEM((G // UB, 2 * UB * T, rows), BF16),
            pltpu.VMEM((G * T, W), F32),
            pltpu.VMEM((B, spd, Uc, W) if raw else (1, 16, 128), BF16),
            pltpu.VMEM((Uc, B * spd, W), BF16),
            pltpu.VMEM((B, Uc * T, W), BF16),
            pltpu.VMEM((2, B, Uc * T, W), BF16),
            pltpu.VMEM((Uc * T, W), F32),
            pltpu.VMEM((Uc * T, W), F32),
            pltpu.VMEM((Uc * T, W), BF16),
            pltpu.VMEM((F, RPF, W), BF16),
            pltpu.VMEM((B, nu, TD, W), F32),
            pltpu.VMEM((nu * T, W), F32),
            pltpu.VMEM((nu * T, W), F32),
            pltpu.VMEM((RPF, W), BF16),
            pltpu.VMEM((Uc * T, W), BF16),
            pltpu.VMEM((B, Uc * T, W), BF16),
            pltpu.VMEM((B, nu, TD, W), F32),
            pltpu.VMEM((F, B, nu, TD, W), F32),
            pltpu.SemaphoreType.DMA((6, B)),
            pltpu.SemaphoreType.DMA((6, B)),
            pltpu.SemaphoreType.DMA((3, F)),
            pltpu.SemaphoreType.DMA((3, F)),
            pltpu.SemaphoreType.DMA((2, B)),
            pltpu.SemaphoreType.DMA((2, B)),
            pltpu.SemaphoreType.DMA((2, B)),
            pltpu.SemaphoreType.DMA((2, B)),
            pltpu.SemaphoreType.DMA,
        ],
        compiler_params=pltpu.CompilerParams(
            collective_id=0, has_side_effects=True, vmem_limit_bytes=56 * 1024 * 1024
        ),
    )(offsets.T, stations.T, counts, facet_model[0], gains, observed.reshape(TD * G, W))
    live = (jnp.arange(TD, dtype=jnp.int32) < counts[0])[:, None, None]
    residual = jnp.where(live, observed - predicted.reshape(TD, G, W), 0.0)
    return (residual, image[None] * (1.0 / (32.0 * G * math.sqrt(T))))


def solution(mesh):
    in_specs = (
        P("facet", "bl", None),
        P("facet", "bl", None, None),
        P("bl", None, None),
        P("bl", None),
        P("bl", None),
        P("bl"),
    )
    out_specs = (P("bl", None, None), P("facet", "bl", None))
    return jax.shard_map(
        functools.partial(per_device, mesh.shape["facet"], mesh.shape["bl"]),
        mesh=mesh, in_specs=in_specs, out_specs=out_specs, check_vma=False,
    )
```

```python
import functools
import math

import jax
import jax.numpy as jnp
from jax import lax
from jax.experimental import pallas as pl
from jax.experimental.pallas import tpu as pltpu
from jax.sharding import PartitionSpec as P

FGRID = 4
F32 = jnp.float32
BF16 = jnp.bfloat16


def cis(k, cells):
    shift = (cells // 4).bit_length() - 1
    turn = (k + cells // 8) >> shift
    x = (k - (turn << shift)).astype(F32) * (2.0 * math.pi / cells)
    y = x * x
    s = x * (1.0 + y * (-1.0 / 6 + y * (1.0 / 120 + y * (-1.0 / 5040 + y * (1.0 / 362880)))))
    c = 1.0 + y * (-0.5 + y * (1.0 / 24 + y * (-1.0 / 720 + y * (1.0 / 40320))))
    odd = (turn & 1) == 1
    cos = jnp.where(odd, s, c)
    sin = jnp.where(odd, c, s)
    cos = jnp.where(((turn + 1) & 2) == 2, -cos, cos)
    sin = jnp.where((turn & 2) == 2, -sin, sin)
    return cos, sin


def kernel(
    dims,
    offsets_ref,
    stations_ref,
    counts_ref,
    model_ref,
    screens_ref,
    obs_ref,
    image_ref,
    pred_ref,
    meta_ref,
    meta_land,
    osend,
    meta_all,
    e2u,
    e1u,
    e1v,
    e2v,
    wv,
    tabv,
    tabu,
    s32,
    scr_raw,
    scr_land,
    sbuf,
    s_land,
    sown,
    gbuf,
    cbuf,
    c_land,
    obs_land,
    obsfull,
    livefull,
    res16,
    r_land,
    rall,
    zsend,
    reso,
    z_send,
    z_recv,
    p_send,
    p_recv,
    w_send,
    w_recv,
    s_send,
    s_recv,
    own_sem,
):
    F, B, T, TD, G, PX, rows, Uc, UB, NT, RPF, nu, per = dims
    N = FGRID * PX
    f = lax.axis_index("facet")
    me = lax.axis_index("bl")
    raw = Uc % 16 == 0
    spd = screens_ref.shape[0 if raw else 1]
    UBT = UB * T
    W = 2 * G
    H = G

    barrier = pltpu.get_barrier_semaphore()
    for k in range(1, B):
        pl.semaphore_signal(
            barrier, inc=1, device_id={"bl": lax.rem(me + k, B)},
            device_id_type=pl.DeviceIdType.MESH,
        )
    for k in range(1, F):
        pl.semaphore_signal(
            barrier, inc=1, device_id={"facet": lax.rem(f + k, F)},
            device_id_type=pl.DeviceIdType.MESH,
        )

    def zcopy(stage, k, src, dst):
        return pltpu.make_async_remote_copy(
            src_ref=src, dst_ref=dst, send_sem=z_send.at[stage, k], recv_sem=z_recv.at[stage, k],
            device_id={"bl": lax.rem(me + k, B)}, device_id_type=pl.DeviceIdType.MESH,
        )

    def pcopy(stage, k, src, dst):
        return pltpu.make_async_remote_copy(
            src_ref=src, dst_ref=dst, send_sem=p_send.at[stage, k], recv_sem=p_recv.at[stage, k],
            device_id={"facet": lax.rem(f + k, F)}, device_id_type=pl.DeviceIdType.MESH,
        )

    def scr_rows(s):
        return pl.ds(pl.multiple_of(s * spd, spd), spd)

    corner_x = (f // FGRID) * PX
    corner_y = (f % FGRID) * PX
    pix_u = lax.broadcasted_iota(jnp.int32, (1, rows), 1) + (corner_x + me * rows)
    pix_v = lax.broadcasted_iota(jnp.int32, (1, PX), 1) + corner_y

    row = lax.broadcasted_iota(jnp.int32, meta_ref.shape, 0)
    col = lax.broadcasted_iota(jnp.int32, meta_ref.shape, 1)
    meta = jnp.where((col == 4) & (row < counts_ref[0]), 1, 0)
    for t in range(TD):
        for j in range(2):
            meta = jnp.where((row == t) & (col == j), offsets_ref[j, t], meta)
            meta = jnp.where((row == t) & (col == j + 2), stations_ref[j, t], meta)
    meta_ref[...] = meta
    for k in range(B):
        c = lax.rem(me + k, B)
        for j in range(nu):
            u = c * Uc + (f // per) * nu + j
            osend[c, j] = obs_ref[pl.ds(u, TD, stride=G), :]

    pl.semaphore_wait(barrier, B + F - 2)

    meta_copies = [zcopy(0, k, meta_ref, meta_land.at[me]) for k in range(1, B)]
    obs_copies = []
    scr_copies = []
    for k in range(1, B):
        c = lax.rem(me + k, B)
        obs_copies.append(zcopy(1, k, osend.at[c], obs_land.at[me]))
        if raw:
            rows_c = pl.ds(pl.multiple_of(c * Uc, Uc), Uc)
            scr_copies.append(zcopy(2, k, screens_ref.at[:, rows_c], scr_raw.at[me]))
        else:
            scr_copies.append(
                zcopy(2, k, screens_ref.at[pl.ds(c * Uc, Uc)], scr_land.at[:, scr_rows(me)])
            )
    for group in (meta_copies, obs_copies, scr_copies[0::2], scr_copies[1::2]):
        for copy in group:
            copy.start()
    if raw:
        own_copy = pltpu.make_async_copy(
            screens_ref.at[:, pl.ds(pl.multiple_of(me * Uc, Uc), Uc)], scr_raw.at[me], own_sem
        )
    else:
        own_copy = pltpu.make_async_copy(
            screens_ref.at[pl.ds(me * Uc, Uc)], scr_land.at[:, scr_rows(me)], own_sem
        )
    own_copy.start()
    meta_land[me] = meta_ref[...]
    obs_land[me] = osend[me]

    cells = lax.broadcasted_iota(jnp.int32, (G, 1), 0)
    cu, su = cis(cells * pix_u, N)
    e2u[0] = cu
    e2u[1] = su
    for j in range(0, PX, 256):
        cv, sv = cis(cells * pix_v[:, j : j + 256], N)
        e2v[0, :, j : j + 256] = cv
        e2v[1, :, j : j + 256] = sv
        wv[:H, j : j + 256] = cv.astype(BF16)
        wv[H:, j : j + 256] = sv.astype(BF16)

    for copy in meta_copies:
        copy.wait()
    for b in range(B):
        meta_all[b * TD : (b + 1) * TD, :] = meta_land[b, :TD, :]
    ou = meta_all[:, 0:1]
    ov = meta_all[:, 1:2]
    c1, s1 = cis(ou * pix_u, N)
    e1u[0] = c1
    e1u[1] = s1
    for j in range(0, PX, 256):
        c1, s1 = cis(ov * pix_v[:, j : j + 256], N)
        e1v[0, :, j : j + 256] = c1
        e1v[1, :, j : j + 256] = s1

    lane = lax.broadcasted_iota(jnp.int32, (1, 2 * G), 1)
    left = lane < G
    sgn = jnp.where(left, 1.0, -1.0).astype(F32)

    def swap(x):
        return pltpu.roll(x, G, 1)

    nchunk = Uc // UB

    def predict(g, carry):
        for j in range(NT):
            t = g * NT + j
            a_c = e1v[0, pl.ds(t, 1), :]
            a_s = e1v[1, pl.ds(t, 1), :]
            tabv[j * W : j * W + H, :] = (a_c * e2v[0] - a_s * e2v[1]).astype(BF16)
            tabv[j * W + H : (j + 1) * W, :] = (a_s * e2v[0] + a_c * e2v[1]).astype(BF16)
        x = lax.dot_general(
            tabv[...], model_ref[...], (((1,), (1,)), ((), ())), preferred_element_type=F32
        ).astype(BF16)
        for j in range(NT):
            t = g * NT + j
            a_c = e1u[0, pl.ds(t, 1), :]
            a_s = e1u[1, pl.ds(t, 1), :]
            top = (a_c * e2u[0] - a_s * e2u[1]).astype(BF16)
            bot = (-(a_s * e2u[0] + a_c * e2u[1])).astype(BF16)
            b = lax.dot_general(
                jnp.concatenate([top, bot], axis=0), x[j * W : (j + 1) * W],
                (((1,), (1,)), ((), ())), preferred_element_type=F32,
            )
            s32[pl.ds(t, G, stride=T), :] = b[:H] * sgn + swap(b[H:])
        return carry

    lax.fori_loop(0, T // NT, predict, 0)

    def image_table(ci, carry):
        for j in range(UB):
            u = ci * UB + j
            e2c = e2u[0, pl.ds(u, 1), :]
            e2s = e2u[1, pl.ds(u, 1), :]
            a_c = e1u[0]
            a_s = e1u[1]
            tabu[ci, j * T : (j + 1) * T, :] = (a_c * e2c - a_s * e2s).astype(BF16)
            tabu[ci, UBT + j * T : UBT + (j + 1) * T, :] = (-(a_s * e2c + a_c * e2s)).astype(BF16)
        return carry

    def chain(side, d):
        to = lax.rem(me + 1, B) if side == 0 else lax.rem(me + B - 1, B)
        return pltpu.make_async_remote_copy(
            src_ref=sbuf.at[d], dst_ref=s_land.at[side, d],
            send_sem=s_send.at[side, d], recv_sem=s_recv.at[side, d],
            device_id={"bl": to}, device_id_type=pl.DeviceIdType.MESH,
        )

    def passes(side, d):
        return me < d if side == 0 else me > d

    def first(side):
        return me == 0 if side == 0 else me == B - 1

    order = []
    for n in range(B):
        for d in (B - 1 - n, n):
            if d not in order:
                order.append(d)
    for d in order:
        sbuf[d] = s32[d * Uc * T : (d + 1) * Uc * T, :].astype(BF16)
        for side in range(2):
            pl.when(first(side) & passes(side, d))(lambda: chain(side, d).start())

    def pass_on(side, d):
        @pl.when(jnp.logical_not(first(side)) & passes(side, d))
        def _():
            chain(side, d).wait_recv()
            sbuf[d] = (sbuf[d].astype(F32) + s_land[side, d].astype(F32)).astype(BF16)
            chain(side, d).start()

    def stand(b):
        if raw:
            block = jnp.swapaxes(scr_raw[b].astype(F32), 0, 1)
            scr_land[:, scr_rows(b), :] = block.astype(BF16)

    own_copy.wait()
    stand(me)
    early = list(range(1, B, 2))
    for n in range(B - 1):
        pass_on(0, B - 1 - n)
        pass_on(1, n)
        if early:
            k = early.pop(0)
            scr_copies[k - 1].wait()
            stand(lax.rem(me + B - k, B))

    for copy in obs_copies:
        copy.wait()
    for j in range(nu):
        for b in range(B):
            obsfull[j * T + b * TD : j * T + (b + 1) * TD, :] = obs_land[b, j]
        livefull[j * T : (j + 1) * T, :] = jnp.broadcast_to(
            meta_all[:, 4:5].astype(F32), (T, 2 * G)
        )

    for k in range(2, B, 2):
        scr_copies[k - 1].wait()
        stand(lax.rem(me + B - k, B))
    stations = lax.broadcasted_iota(jnp.int32, (1, B * spd), 1)
    pick = jnp.concatenate([meta_all[:, 2:3], meta_all[:, 3:4]], axis=0) == stations
    pick = jnp.where(pick, 1.0, 0.0).astype(BF16)

    def gains(u, carry):
        both = jnp.dot(pick, scr_land[u], preferred_element_type=F32)
        p = both[:T]
        q = both[T:]
        qsw = swap(q)
        g = p * jnp.where(left, q, qsw) + swap(p) * jnp.where(left, qsw, -q)
        gbuf[pl.ds(pl.multiple_of(u * T, T), T), :] = g
        return carry

    lax.fori_loop(0, Uc, gains, 0, unroll=4)

    sown[...] = sbuf[me].astype(F32)
    for side in range(2):

        @pl.when(jnp.logical_not(first(side)))
        def _(side=side):
            chain(side, me).wait_recv()
            sown[...] += s_land[side, me].astype(F32)

    def contribution(u, carry):
        r = pl.ds(pl.multiple_of(u * T, T), T)
        s = sown[r, :]
        g = gbuf[r, :]
        gsw = swap(g)
        out = s * jnp.where(left, g, gsw) + swap(s) * jnp.where(left, -gsw, g)
        cbuf[r, :] = out.astype(BF16)
        return carry

    lax.fori_loop(0, Uc, contribution, 0, unroll=4)

    def piece(i):
        return pl.ds(pl.multiple_of(i * RPF, RPF), RPF)

    c_copies = [
        pcopy(0, k, cbuf.at[piece(lax.rem(f + k, F))], c_land.at[f]) for k in range(1, F)
    ]
    for copy in c_copies:
        copy.start()
    lax.fori_loop(0, G // UB, image_table, 0)
    total = cbuf[piece(f), :].astype(F32)
    for copy in c_copies:
        copy.wait()
    for k in range(1, F):
        total = total + c_land[lax.rem(f + k, F)].astype(F32)
    span = pl.ds(pl.multiple_of((f % per) * RPF, RPF), RPF)
    res = jnp.where(livefull[span, :] > 0.5, obsfull[span, :] - total, 0.0)
    r_land[piece(f), :] = res.astype(BF16)
    res16[...] = res.astype(BF16)
    r_copies = [pcopy(1, k, res16, r_land.at[piece(f)]) for k in range(1, F)]
    for copy in r_copies:
        copy.start()
    if per > 1:
        obsfull[...] = jnp.zeros_like(obsfull)
    obsfull[span, :] = total
    for j in range(nu):
        for b in range(B):
            zsend[b, j] = obsfull[j * T + b * TD : j * T + (b + 1) * TD, :]
    reso[f, me] = zsend[me]
    for copy in r_copies:
        copy.wait()

    def weigh(u, carry):
        r = pl.ds(pl.multiple_of(u * T, T), T)
        x = r_land[r, :].astype(F32)
        g = gbuf[r, :]
        gsw = swap(g)
        out = x * jnp.where(left, g, gsw) + swap(x) * jnp.where(left, gsw, -g)
        rall[me, r, :] = out.astype(BF16)
        return carry

    lax.fori_loop(0, Uc, weigh, 0, unroll=4)

    def right(n):
        block = jnp.maximum(me - n, 0)
        return pltpu.make_async_remote_copy(
            src_ref=rall.at[block], dst_ref=rall.at[block],
            send_sem=w_send.at[0, n], recv_sem=w_recv.at[0, n],
            device_id={"bl": lax.rem(me + 1, B)}, device_id_type=pl.DeviceIdType.MESH,
        )

    def left_(n):
        block = jnp.minimum(me + n, B - 1)
        return pltpu.make_async_remote_copy(
            src_ref=rall.at[block], dst_ref=rall.at[block],
            send_sem=w_send.at[1, n], recv_sem=w_recv.at[1, n],
            device_id={"bl": lax.rem(me + B - 1, B)}, device_id_type=pl.DeviceIdType.MESH,
        )

    def sends_right(n):
        return (me - n >= 0) & (me + 1 < B)

    def sends_left(n):
        return (me + n < B) & (me >= 1)

    pl.when(sends_right(0))(lambda: right(0).start())
    pl.when(sends_left(0))(lambda: left_(0).start())
    z_copies = [
        zcopy(5, k, zsend.at[lax.rem(me + k, B)], reso.at[f, me]) for k in range(1, B)
    ]
    for copy in z_copies:
        copy.start()

    image_ref[...] = jnp.zeros_like(image_ref)

    def image(src):
        def body(i, carry):
            ci = src * nchunk + i
            r = rall[src, pl.ds(pl.multiple_of(i * UBT, UBT), UBT), :].astype(F32)
            both = jnp.concatenate([(r * sgn).astype(BF16), swap(r).astype(BF16)], axis=0)
            prod = jnp.dot(both, wv[...], preferred_element_type=F32)
            tops, bots = [], []
            for j in range(UB):
                pc = prod[j * T : (j + 1) * T]
                ps = prod[UBT + j * T : UBT + (j + 1) * T]
                tops.append((pc * e1v[0] - ps * e1v[1]).astype(BF16))
                bots.append((ps * e1v[0] + pc * e1v[1]).astype(BF16))
            q2 = jnp.concatenate(tops + bots, axis=0)
            image_ref[...] += lax.dot_general(
                tabu[ci], q2, (((0,), (0,)), ((), ())), preferred_element_type=F32
            )
            return carry

        lax.fori_loop(0, nchunk, body, 0)

    image(me)
    for copy in z_copies:
        copy.wait()
    o_copies = [pcopy(2, k, reso.at[f], reso.at[f]) for k in range(1, F)]
    for copy in o_copies:
        copy.start()
    for n in range(B - 1):
        if n == B - 2:
            for copy in o_copies:
                copy.wait()
            group = (me * TD) // RPF if per > 1 else 0
            for g in range(F // per):
                for c in range(B):
                    for j in range(nu):
                        u = c * Uc + g * nu + j
                        pred_ref[pl.ds(u, TD, stride=G), :] = reso[g * per + group, c, j]
        pl.when(me - 1 - n >= 0)(lambda n=n: right(n).wait_recv())
        if n + 1 < B - 1:
            pl.when(sends_right(n + 1))(lambda n=n: right(n + 1).start())
        pl.when(me + 1 + n < B)(lambda n=n: left_(n).wait_recv())
        if n + 1 < B - 1:
            pl.when(sends_left(n + 1))(lambda n=n: left_(n + 1).start())

        def arrived(side, carry, n=n):
            src = jnp.where(side == 0, me - 1 - n, me + 1 + n)
            pl.when((src >= 0) & (src < B))(lambda: image(src))
            return carry

        lax.fori_loop(0, 2, arrived, 0)
    for n in range(B - 1):
        pl.when(sends_right(n))(lambda n=n: right(n).wait_send())
        pl.when(sends_left(n))(lambda n=n: left_(n).wait_send())
    for d in range(B):
        for side in range(2):
            pl.when(passes(side, d))(lambda: chain(side, d).wait_send())


def per_device(F, B, facet_model, screens, observed, offsets, stations, counts):
    TD, G = observed.shape[0], observed.shape[1]
    PX = facet_model.shape[2]
    rows = facet_model.shape[1]
    spd = screens.shape[1]
    T = TD * B
    Uc = G // B
    UB = max(1, min(Uc, 384 // T))
    NT = 4 if T % 4 == 0 else 1
    RPF = Uc * T // F
    nu = max(1, RPF // T)
    per = max(1, T // RPF)
    dims = (F, B, T, TD, G, PX, rows, Uc, UB, NT, RPF, nu, per)
    tdp = -(-TD // 8) * 8
    raw = Uc % 16 == 0
    gains = screens[0] if raw else jnp.transpose(screens[0], (1, 0, 2))
    W = 2 * G
    vmem = pl.BlockSpec(memory_space=pltpu.VMEM)
    smem = pl.BlockSpec(memory_space=pltpu.SMEM)
    image, predicted = pl.pallas_call(
        functools.partial(kernel, dims),
        out_shape=(
            jax.ShapeDtypeStruct((rows, PX), F32),
            jax.ShapeDtypeStruct((TD * G, W), F32),
        ),
        in_specs=[smem] * 3 + [vmem] * 3,
        out_specs=(vmem, vmem),
        scratch_shapes=[
            pltpu.VMEM((tdp, 128), jnp.int32),
            pltpu.VMEM((B, tdp, 128), jnp.int32),
            pltpu.VMEM((B, nu, TD, W), F32),
            pltpu.VMEM((T, 128), jnp.int32),
            pltpu.VMEM((2, G, rows), F32),
            pltpu.VMEM((2, T, rows), F32),
            pltpu.VMEM((2, T, PX), F32),
            pltpu.VMEM((2, G, PX), F32),
            pltpu.VMEM((W, PX), BF16),
            pltpu.VMEM((NT * W, PX), BF16),
            pltpu.VMEM((G // UB, 2 * UB * T, rows), BF16),
            pltpu.VMEM((G * T, W), F32),
            pltpu.VMEM((B, spd, Uc, W) if raw else (1, 16, 128), BF16),
            pltpu.VMEM((Uc, B * spd, W), BF16),
            pltpu.VMEM((B, Uc * T, W), BF16),
            pltpu.VMEM((2, B, Uc * T, W), BF16),
            pltpu.VMEM((Uc * T, W), F32),
            pltpu.VMEM((Uc * T, W), F32),
            pltpu.VMEM((Uc * T, W), BF16),
            pltpu.VMEM((F, RPF, W), BF16),
            pltpu.VMEM((B, nu, TD, W), F32),
            pltpu.VMEM((nu * T, W), F32),
            pltpu.VMEM((nu * T, W), F32),
            pltpu.VMEM((RPF, W), BF16),
            pltpu.VMEM((Uc * T, W), BF16),
            pltpu.VMEM((B, Uc * T, W), BF16),
            pltpu.VMEM((B, nu, TD, W), F32),
            pltpu.VMEM((F, B, nu, TD, W), F32),
            pltpu.SemaphoreType.DMA((6, B)),
            pltpu.SemaphoreType.DMA((6, B)),
            pltpu.SemaphoreType.DMA((3, F)),
            pltpu.SemaphoreType.DMA((3, F)),
            pltpu.SemaphoreType.DMA((2, B)),
            pltpu.SemaphoreType.DMA((2, B)),
            pltpu.SemaphoreType.DMA((2, B)),
            pltpu.SemaphoreType.DMA((2, B)),
            pltpu.SemaphoreType.DMA,
        ],
        compiler_params=pltpu.CompilerParams(
            collective_id=0, has_side_effects=True, vmem_limit_bytes=56 * 1024 * 1024
        ),
    )(offsets.T, stations.T, counts, facet_model[0], gains, observed.reshape(TD * G, W))
    live = (jnp.arange(TD, dtype=jnp.int32) < counts[0])[:, None, None]
    residual = jnp.where(live, observed - predicted.reshape(TD, G, W), 0.0)
    return (residual, image[None] * (1.0 / (32.0 * G * math.sqrt(T))))


def solution(mesh):
    in_specs = (
        P("facet", "bl", None),
        P("facet", "bl", None, None),
        P("bl", None, None),
        P("bl", None),
        P("bl", None),
        P("bl"),
    )
    out_specs = (P("bl", None, None), P("facet", "bl", None))
    return jax.shard_map(
        functools.partial(per_device, mesh.shape["facet"], mesh.shape["bl"]),
        mesh=mesh, in_specs=in_specs, out_specs=out_specs, check_vma=False,
    )
```

```python
import functools
import math

import jax
import jax.numpy as jnp
from jax import lax
from jax.experimental import pallas as pl
from jax.experimental.pallas import tpu as pltpu
from jax.sharding import PartitionSpec as P

FGRID = 4
F32 = jnp.float32
BF16 = jnp.bfloat16


def cis(k, cells):
    shift = (cells // 4).bit_length() - 1
    turn = (k + cells // 8) >> shift
    x = (k - (turn << shift)).astype(F32) * (2.0 * math.pi / cells)
    y = x * x
    s = x * (1.0 + y * (-1.0 / 6 + y * (1.0 / 120 + y * (-1.0 / 5040 + y * (1.0 / 362880)))))
    c = 1.0 + y * (-0.5 + y * (1.0 / 24 + y * (-1.0 / 720 + y * (1.0 / 40320))))
    odd = (turn & 1) == 1
    cos = jnp.where(odd, s, c)
    sin = jnp.where(odd, c, s)
    cos = jnp.where(((turn + 1) & 2) == 2, -cos, cos)
    sin = jnp.where((turn & 2) == 2, -sin, sin)
    return cos, sin


def kernel(
    dims,
    offsets_ref,
    stations_ref,
    counts_ref,
    model_ref,
    screens_ref,
    obs_ref,
    image_ref,
    pred_ref,
    meta_ref,
    meta_land,
    osend,
    meta_all,
    e2u,
    e1u,
    e1v,
    e2v,
    wv,
    tabv,
    tabu,
    s32,
    scr_raw,
    scr_land,
    sbuf,
    s_land,
    sown,
    gbuf,
    cbuf,
    c_land,
    obs_land,
    obsfull,
    livefull,
    res16,
    r_land,
    rall,
    zsend,
    reso,
    z_send,
    z_recv,
    p_send,
    p_recv,
    w_send,
    w_recv,
    s_send,
    s_recv,
    own_sem,
):
    F, B, T, TD, G, PX, rows, Uc, UB, NT, RPF, nu, per = dims
    N = FGRID * PX
    f = lax.axis_index("facet")
    me = lax.axis_index("bl")
    raw = Uc % 16 == 0
    spd = screens_ref.shape[0 if raw else 1]
    UBT = UB * T
    W = 2 * G
    H = G

    barrier = pltpu.get_barrier_semaphore()
    for k in range(1, B):
        pl.semaphore_signal(
            barrier, inc=1, device_id={"bl": lax.rem(me + k, B)},
            device_id_type=pl.DeviceIdType.MESH,
        )
    for k in range(1, F):
        pl.semaphore_signal(
            barrier, inc=1, device_id={"facet": lax.rem(f + k, F)},
            device_id_type=pl.DeviceIdType.MESH,
        )

    def zcopy(stage, k, src, dst):
        return pltpu.make_async_remote_copy(
            src_ref=src, dst_ref=dst, send_sem=z_send.at[stage, k], recv_sem=z_recv.at[stage, k],
            device_id={"bl": lax.rem(me + k, B)}, device_id_type=pl.DeviceIdType.MESH,
        )

    def pcopy(stage, k, src, dst):
        return pltpu.make_async_remote_copy(
            src_ref=src, dst_ref=dst, send_sem=p_send.at[stage, k], recv_sem=p_recv.at[stage, k],
            device_id={"facet": lax.rem(f + k, F)}, device_id_type=pl.DeviceIdType.MESH,
        )

    def scr_rows(s):
        return pl.ds(pl.multiple_of(s * spd, spd), spd)

    corner_x = (f // FGRID) * PX
    corner_y = (f % FGRID) * PX
    pix_u = lax.broadcasted_iota(jnp.int32, (1, rows), 1) + (corner_x + me * rows)
    pix_v = lax.broadcasted_iota(jnp.int32, (1, PX), 1) + corner_y

    row = lax.broadcasted_iota(jnp.int32, meta_ref.shape, 0)
    col = lax.broadcasted_iota(jnp.int32, meta_ref.shape, 1)
    meta = jnp.where((col == 4) & (row < counts_ref[0]), 1, 0)
    for t in range(TD):
        for j in range(2):
            meta = jnp.where((row == t) & (col == j), offsets_ref[j, t], meta)
            meta = jnp.where((row == t) & (col == j + 2), stations_ref[j, t], meta)
    meta_ref[...] = meta
    for k in range(B):
        c = lax.rem(me + k, B)
        for j in range(nu):
            u = c * Uc + (f // per) * nu + j
            osend[c, j] = obs_ref[pl.ds(u, TD, stride=G), :]

    pl.semaphore_wait(barrier, B + F - 2)

    meta_copies = [zcopy(0, k, meta_ref, meta_land.at[me]) for k in range(1, B)]
    obs_copies = []
    scr_copies = []
    for k in range(1, B):
        c = lax.rem(me + k, B)
        obs_copies.append(zcopy(1, k, osend.at[c], obs_land.at[me]))
        if raw:
            rows_c = pl.ds(pl.multiple_of(c * Uc, Uc), Uc)
            scr_copies.append(zcopy(2, k, screens_ref.at[:, rows_c], scr_raw.at[me]))
        else:
            scr_copies.append(
                zcopy(2, k, screens_ref.at[pl.ds(c * Uc, Uc)], scr_land.at[:, scr_rows(me)])
            )
    for group in (meta_copies, obs_copies, scr_copies[0::2], scr_copies[1::2]):
        for copy in group:
            copy.start()
    if raw:
        own_copy = pltpu.make_async_copy(
            screens_ref.at[:, pl.ds(pl.multiple_of(me * Uc, Uc), Uc)], scr_raw.at[me], own_sem
        )
    else:
        own_copy = pltpu.make_async_copy(
            screens_ref.at[pl.ds(me * Uc, Uc)], scr_land.at[:, scr_rows(me)], own_sem
        )
    own_copy.start()
    meta_land[me] = meta_ref[...]
    obs_land[me] = osend[me]

    cells = lax.broadcasted_iota(jnp.int32, (G, 1), 0)
    cu, su = cis(cells * pix_u, N)
    e2u[0] = cu
    e2u[1] = su
    for j in range(0, PX, 256):
        cv, sv = cis(cells * pix_v[:, j : j + 256], N)
        e2v[0, :, j : j + 256] = cv
        e2v[1, :, j : j + 256] = sv
        wv[:H, j : j + 256] = cv.astype(BF16)
        wv[H:, j : j + 256] = sv.astype(BF16)

    for copy in meta_copies:
        copy.wait()
    for b in range(B):
        meta_all[b * TD : (b + 1) * TD, :] = meta_land[b, :TD, :]
    ou = meta_all[:, 0:1]
    ov = meta_all[:, 1:2]
    c1, s1 = cis(ou * pix_u, N)
    e1u[0] = c1
    e1u[1] = s1
    for j in range(0, PX, 256):
        c1, s1 = cis(ov * pix_v[:, j : j + 256], N)
        e1v[0, :, j : j + 256] = c1
        e1v[1, :, j : j + 256] = s1

    lane = lax.broadcasted_iota(jnp.int32, (1, 2 * G), 1)
    left = lane < G
    sgn = jnp.where(left, 1.0, -1.0).astype(F32)

    def swap(x):
        return pltpu.roll(x, G, 1)

    nchunk = Uc // UB

    def predict(g, carry):
        for j in range(NT):
            t = g * NT + j
            a_c = e1v[0, pl.ds(t, 1), :]
            a_s = e1v[1, pl.ds(t, 1), :]
            tabv[j * W : j * W + H, :] = (a_c * e2v[0] - a_s * e2v[1]).astype(BF16)
            tabv[j * W + H : (j + 1) * W, :] = (a_s * e2v[0] + a_c * e2v[1]).astype(BF16)
        x = lax.dot_general(
            tabv[...], model_ref[...], (((1,), (1,)), ((), ())), preferred_element_type=F32
        ).astype(BF16)
        for j in range(NT):
            t = g * NT + j
            a_c = e1u[0, pl.ds(t, 1), :]
            a_s = e1u[1, pl.ds(t, 1), :]
            top = (a_c * e2u[0] - a_s * e2u[1]).astype(BF16)
            bot = (-(a_s * e2u[0] + a_c * e2u[1])).astype(BF16)
            b = lax.dot_general(
                jnp.concatenate([top, bot], axis=0), x[j * W : (j + 1) * W],
                (((1,), (1,)), ((), ())), preferred_element_type=F32,
            )
            s32[pl.ds(t, G, stride=T), :] = b[:H] * sgn + swap(b[H:])
        return carry

    lax.fori_loop(0, T // NT, predict, 0)

    def image_table(ci, carry):
        for j in range(UB):
            u = ci * UB + j
            e2c = e2u[0, pl.ds(u, 1), :]
            e2s = e2u[1, pl.ds(u, 1), :]
            a_c = e1u[0]
            a_s = e1u[1]
            tabu[ci, j * T : (j + 1) * T, :] = (a_c * e2c - a_s * e2s).astype(BF16)
            tabu[ci, UBT + j * T : UBT + (j + 1) * T, :] = (-(a_s * e2c + a_c * e2s)).astype(BF16)
        return carry

    def chain(side, d):
        to = lax.rem(me + 1, B) if side == 0 else lax.rem(me + B - 1, B)
        return pltpu.make_async_remote_copy(
            src_ref=sbuf.at[d], dst_ref=s_land.at[side, d],
            send_sem=s_send.at[side, d], recv_sem=s_recv.at[side, d],
            device_id={"bl": to}, device_id_type=pl.DeviceIdType.MESH,
        )

    def passes(side, d):
        return me < d if side == 0 else me > d

    def first(side):
        return me == 0 if side == 0 else me == B - 1

    order = []
    for n in range(B):
        for d in (B - 1 - n, n):
            if d not in order:
                order.append(d)
    for d in order:
        sbuf[d] = s32[d * Uc * T : (d + 1) * Uc * T, :].astype(BF16)
        for side in range(2):
            pl.when(first(side) & passes(side, d))(lambda: chain(side, d).start())

    def pass_on(side, d):
        @pl.when(jnp.logical_not(first(side)) & passes(side, d))
        def _():
            chain(side, d).wait_recv()
            sbuf[d] = (sbuf[d].astype(F32) + s_land[side, d].astype(F32)).astype(BF16)
            chain(side, d).start()

    def stand(b):
        if raw:
            block = jnp.swapaxes(scr_raw[b].astype(F32), 0, 1)
            scr_land[:, scr_rows(b), :] = block.astype(BF16)

    own_copy.wait()
    stand(me)
    early = list(range(1, B, 2))
    for n in range(B - 1):
        pass_on(0, B - 1 - n)
        pass_on(1, n)
        if early:
            k = early.pop(0)
            scr_copies[k - 1].wait()
            stand(lax.rem(me + B - k, B))

    for copy in obs_copies:
        copy.wait()
    for j in range(nu):
        for b in range(B):
            obsfull[j * T + b * TD : j * T + (b + 1) * TD, :] = obs_land[b, j]
        livefull[j * T : (j + 1) * T, :] = jnp.broadcast_to(
            meta_all[:, 4:5].astype(F32), (T, 2 * G)
        )

    for k in range(2, B, 2):
        scr_copies[k - 1].wait()
        stand(lax.rem(me + B - k, B))
    stations = lax.broadcasted_iota(jnp.int32, (1, B * spd), 1)
    pick = jnp.concatenate([meta_all[:, 2:3], meta_all[:, 3:4]], axis=0) == stations
    pick = jnp.where(pick, 1.0, 0.0).astype(BF16)

    def gains(u, carry):
        both = jnp.dot(pick, scr_land[u], preferred_element_type=F32)
        p = both[:T]
        q = both[T:]
        qsw = swap(q)
        g = p * jnp.where(left, q, qsw) + swap(p) * jnp.where(left, qsw, -q)
        gbuf[pl.ds(pl.multiple_of(u * T, T), T), :] = g
        return carry

    lax.fori_loop(0, Uc, gains, 0, unroll=4)

    sown[...] = sbuf[me].astype(F32)
    for side in range(2):

        @pl.when(jnp.logical_not(first(side)))
        def _(side=side):
            chain(side, me).wait_recv()
            sown[...] += s_land[side, me].astype(F32)

    def contribution(u, carry):
        r = pl.ds(pl.multiple_of(u * T, T), T)
        s = sown[r, :]
        g = gbuf[r, :]
        gsw = swap(g)
        out = s * jnp.where(left, g, gsw) + swap(s) * jnp.where(left, -gsw, g)
        cbuf[r, :] = out.astype(BF16)
        return carry

    lax.fori_loop(0, Uc, contribution, 0, unroll=4)

    def piece(i):
        return pl.ds(pl.multiple_of(i * RPF, RPF), RPF)

    c_copies = [
        pcopy(0, k, cbuf.at[piece(lax.rem(f + k, F))], c_land.at[f]) for k in range(1, F)
    ]
    for copy in c_copies:
        copy.start()
    lax.fori_loop(0, G // UB, image_table, 0)
    total = cbuf[piece(f), :].astype(F32)
    for copy in c_copies:
        copy.wait()
    for k in range(1, F):
        total = total + c_land[lax.rem(f + k, F)].astype(F32)
    span = pl.ds(pl.multiple_of((f % per) * RPF, RPF), RPF)
    res = jnp.where(livefull[span, :] > 0.5, obsfull[span, :] - total, 0.0)
    r_land[piece(f), :] = res.astype(BF16)
    res16[...] = res.astype(BF16)
    r_copies = [pcopy(1, k, res16, r_land.at[piece(f)]) for k in range(1, F)]
    for copy in r_copies:
        copy.start()
    if per > 1:
        obsfull[...] = jnp.zeros_like(obsfull)
    obsfull[span, :] = total
    for j in range(nu):
        for b in range(B):
            zsend[b, j] = obsfull[j * T + b * TD : j * T + (b + 1) * TD, :]
    reso[f, me] = zsend[me]
    for copy in r_copies:
        copy.wait()

    def weigh(u, carry):
        r = pl.ds(pl.multiple_of(u * T, T), T)
        x = r_land[r, :].astype(F32)
        g = gbuf[r, :]
        gsw = swap(g)
        out = x * jnp.where(left, g, gsw) + swap(x) * jnp.where(left, gsw, -g)
        rall[me, r, :] = out.astype(BF16)
        return carry

    lax.fori_loop(0, Uc, weigh, 0, unroll=4)

    def right(n):
        block = jnp.maximum(me - n, 0)
        return pltpu.make_async_remote_copy(
            src_ref=rall.at[block], dst_ref=rall.at[block],
            send_sem=w_send.at[0, n], recv_sem=w_recv.at[0, n],
            device_id={"bl": lax.rem(me + 1, B)}, device_id_type=pl.DeviceIdType.MESH,
        )

    def left_(n):
        block = jnp.minimum(me + n, B - 1)
        return pltpu.make_async_remote_copy(
            src_ref=rall.at[block], dst_ref=rall.at[block],
            send_sem=w_send.at[1, n], recv_sem=w_recv.at[1, n],
            device_id={"bl": lax.rem(me + B - 1, B)}, device_id_type=pl.DeviceIdType.MESH,
        )

    def sends_right(n):
        return (me - n >= 0) & (me + 1 < B)

    def sends_left(n):
        return (me + n < B) & (me >= 1)

    pl.when(sends_right(0))(lambda: right(0).start())
    pl.when(sends_left(0))(lambda: left_(0).start())
    z_copies = [
        zcopy(5, k, zsend.at[lax.rem(me + k, B)], reso.at[f, me]) for k in range(1, B)
    ]
    for copy in z_copies:
        copy.start()

    image_ref[...] = jnp.zeros_like(image_ref)

    def image(src):
        def body(i, carry):
            ci = src * nchunk + i
            r = rall[src, pl.ds(pl.multiple_of(i * UBT, UBT), UBT), :].astype(F32)
            both = jnp.concatenate([(r * sgn).astype(BF16), swap(r).astype(BF16)], axis=0)
            prod = jnp.dot(both, wv[...], preferred_element_type=F32)
            tops, bots = [], []
            for j in range(UB):
                pc = prod[j * T : (j + 1) * T]
                ps = prod[UBT + j * T : UBT + (j + 1) * T]
                tops.append((pc * e1v[0] - ps * e1v[1]).astype(BF16))
                bots.append((ps * e1v[0] + pc * e1v[1]).astype(BF16))
            q2 = jnp.concatenate(tops + bots, axis=0)
            image_ref[...] += lax.dot_general(
                tabu[ci], q2, (((0,), (0,)), ((), ())), preferred_element_type=F32
            )
            return carry

        lax.fori_loop(0, nchunk, body, 0, unroll=2 if nchunk % 2 == 0 else 1)

    image(me)
    o_copies = [pcopy(2, k, reso.at[f], reso.at[f]) for k in range(1, F)]
    for n in range(B - 1):
        if n == B - 2:
            for copy in o_copies:
                copy.wait()
            group = (me * TD) // RPF if per > 1 else 0
            for g in range(F // per):
                for c in range(B):
                    for j in range(nu):
                        u = c * Uc + g * nu + j
                        pred_ref[pl.ds(u, TD, stride=G), :] = reso[g * per + group, c, j]
        pl.when(me - 1 - n >= 0)(lambda n=n: right(n).wait_recv())
        if n + 1 < B - 1:
            pl.when(sends_right(n + 1))(lambda n=n: right(n + 1).start())
        pl.when(me + 1 + n < B)(lambda n=n: left_(n).wait_recv())
        if n + 1 < B - 1:
            pl.when(sends_left(n + 1))(lambda n=n: left_(n + 1).start())
        if n == 0:
            for copy in z_copies:
                copy.wait()
            for copy in o_copies:
                copy.start()

        def arrived(side, carry, n=n):
            src = jnp.where(side == 0, me - 1 - n, me + 1 + n)
            pl.when((src >= 0) & (src < B))(lambda: image(src))
            return carry

        lax.fori_loop(0, 2, arrived, 0)
    for n in range(B - 1):
        pl.when(sends_right(n))(lambda n=n: right(n).wait_send())
        pl.when(sends_left(n))(lambda n=n: left_(n).wait_send())
    for d in range(B):
        for side in range(2):
            pl.when(passes(side, d))(lambda: chain(side, d).wait_send())


def per_device(F, B, facet_model, screens, observed, offsets, stations, counts):
    TD, G = observed.shape[0], observed.shape[1]
    PX = facet_model.shape[2]
    rows = facet_model.shape[1]
    spd = screens.shape[1]
    T = TD * B
    Uc = G // B
    UB = max(1, min(Uc, 384 // T))
    NT = 4 if T % 4 == 0 else 1
    RPF = Uc * T // F
    nu = max(1, RPF // T)
    per = max(1, T // RPF)
    dims = (F, B, T, TD, G, PX, rows, Uc, UB, NT, RPF, nu, per)
    tdp = -(-TD // 8) * 8
    raw = Uc % 16 == 0
    gains = screens[0] if raw else jnp.transpose(screens[0], (1, 0, 2))
    W = 2 * G
    vmem = pl.BlockSpec(memory_space=pltpu.VMEM)
    smem = pl.BlockSpec(memory_space=pltpu.SMEM)
    image, predicted = pl.pallas_call(
        functools.partial(kernel, dims),
        out_shape=(
            jax.ShapeDtypeStruct((rows, PX), F32),
            jax.ShapeDtypeStruct((TD * G, W), F32),
        ),
        in_specs=[smem] * 3 + [vmem] * 3,
        out_specs=(vmem, vmem),
        scratch_shapes=[
            pltpu.VMEM((tdp, 128), jnp.int32),
            pltpu.VMEM((B, tdp, 128), jnp.int32),
            pltpu.VMEM((B, nu, TD, W), F32),
            pltpu.VMEM((T, 128), jnp.int32),
            pltpu.VMEM((2, G, rows), F32),
            pltpu.VMEM((2, T, rows), F32),
            pltpu.VMEM((2, T, PX), F32),
            pltpu.VMEM((2, G, PX), F32),
            pltpu.VMEM((W, PX), BF16),
            pltpu.VMEM((NT * W, PX), BF16),
            pltpu.VMEM((G // UB, 2 * UB * T, rows), BF16),
            pltpu.VMEM((G * T, W), F32),
            pltpu.VMEM((B, spd, Uc, W) if raw else (1, 16, 128), BF16),
            pltpu.VMEM((Uc, B * spd, W), BF16),
            pltpu.VMEM((B, Uc * T, W), BF16),
            pltpu.VMEM((2, B, Uc * T, W), BF16),
            pltpu.VMEM((Uc * T, W), F32),
            pltpu.VMEM((Uc * T, W), F32),
            pltpu.VMEM((Uc * T, W), BF16),
            pltpu.VMEM((F, RPF, W), BF16),
            pltpu.VMEM((B, nu, TD, W), F32),
            pltpu.VMEM((nu * T, W), F32),
            pltpu.VMEM((nu * T, W), F32),
            pltpu.VMEM((RPF, W), BF16),
            pltpu.VMEM((Uc * T, W), BF16),
            pltpu.VMEM((B, Uc * T, W), BF16),
            pltpu.VMEM((B, nu, TD, W), F32),
            pltpu.VMEM((F, B, nu, TD, W), F32),
            pltpu.SemaphoreType.DMA((6, B)),
            pltpu.SemaphoreType.DMA((6, B)),
            pltpu.SemaphoreType.DMA((3, F)),
            pltpu.SemaphoreType.DMA((3, F)),
            pltpu.SemaphoreType.DMA((2, B)),
            pltpu.SemaphoreType.DMA((2, B)),
            pltpu.SemaphoreType.DMA((2, B)),
            pltpu.SemaphoreType.DMA((2, B)),
            pltpu.SemaphoreType.DMA,
        ],
        compiler_params=pltpu.CompilerParams(
            collective_id=0, has_side_effects=True, vmem_limit_bytes=56 * 1024 * 1024
        ),
    )(offsets.T, stations.T, counts, facet_model[0], gains, observed.reshape(TD * G, W))
    live = (jnp.arange(TD, dtype=jnp.int32) < counts[0])[:, None, None]
    residual = jnp.where(live, observed - predicted.reshape(TD, G, W), 0.0)
    return (residual, image[None] * (1.0 / (32.0 * G * math.sqrt(T))))


def solution(mesh):
    in_specs = (
        P("facet", "bl", None),
        P("facet", "bl", None, None),
        P("bl", None, None),
        P("bl", None),
        P("bl", None),
        P("bl"),
    )
    out_specs = (P("bl", None, None), P("facet", "bl", None))
    return jax.shard_map(
        functools.partial(per_device, mesh.shape["facet"], mesh.shape["bl"]),
        mesh=mesh, in_specs=in_specs, out_specs=out_specs, check_vma=False,
    )
```
